128 devices in a mesh: gx: 8 (over x, core), gy: 16 (over z, y).
Axes of the slice: x: 4, y: 4, z: 4, core: 2. Of those that a mesh axis runs over, the one named last changes fastest.
Arguments:
- features: bfloat16 [128, 256, 64, 128], P('gx', 'gy'), may hold values from -6 to 6
- occupancy: int32 [128, 256, 64], P('gx', 'gy'), may hold values 0 or 1
- weight: bfloat16 [27, 128, 256], replicated, may hold values from -0.109375 to 0.109375
- owner: int32 [8, 16, 32], P('gx', 'gy'), may hold values from 0 to 15, as said below
- cotangent: bfloat16 [8, 16, 48, 16384], P('gx', 'gy'), may hold values from -6 to 6
Outputs:
- owned_output: bfloat16 [8, 16, 48, 16384], P('gx', 'gy')
- grad_input: bfloat16 [128, 256, 64, 128], P('gx', 'gy')
- grad_weight: float32 [27, 128, 256], replicated
The draws below stay inside these ranges and needn't reach their ends.
Inputs may be any that keep to these rules, and one draw needn't show every extreme that they name: Each device sends at most 3 of its 32 output bricks to any one owner; one owner receives exactly 3 bricks from every device of its gx index.
All inputs are finite; a program needn't handle non-finite values. No bound on the sum of `occupancy` on one device may be relied on, other than what follows from the above.
Results may differ from the reference program's by a relative error of at most 0.0035.
Values may be sent and summed in bfloat16 or wider, within the bound.
A program may use at most 192 MiB of HBM per device.

```python
import jax
import jax.numpy as jnp

C_IN = 128
C_OUT = 256
KV = 27
SX = 16
SY = 16
SZ = 64
NX = 128
NY = 256
NZ = 64
BRICKS_DEV = 32
CAP = 3
N_GX = 8
N_GY = 16


def draw_owner(key, part):
    key = jax.random.fold_in(key, 11)
    key_main, key_rest = jax.random.split(key)
    chosen = jax.random.randint(key_main, (), 0, N_GY)
    others = jnp.arange(N_GY - 1, dtype=jnp.int32)
    others = others + (others >= chosen).astype(jnp.int32)
    others = jnp.repeat(others, CAP)

    def single(one_key):
        key_pool, key_order = jax.random.split(one_key)
        mixed = jax.random.permutation(key_pool, others)
        listing = jnp.concatenate([jnp.full((CAP,), chosen, jnp.int32), mixed[:BRICKS_DEV - CAP]])
        return jax.random.permutation(key_order, listing)
    keys = jax.random.split(key_rest, N_GX * N_GY)
    return jax.vmap(single)(keys).reshape(N_GX, N_GY, BRICKS_DEV).astype(jnp.int32)


def with_ends(drawn, own_key, least, high):
    longest = drawn.shape.index(max(drawn.shape))
    spots = []
    for shift in (0, 1):
        where = [jax.random.randint(jax.random.fold_in(own_key, axis), (), 0, length) for axis, length in enumerate(drawn.shape)]
        where[longest] = (where[longest] + shift) % drawn.shape[longest]
        spots.append(tuple(where))
    return drawn.at[spots[0]].set(least).at[spots[1]].set(high)


def level_of(own_key, shape, shards, smallest, high):
    def one(position, blocks):
        draws = jax.random.uniform(jax.random.fold_in(jax.random.fold_in(own_key, 6), position), (blocks,), jnp.float32, smallest / len(shards), high / len(shards))
        return jnp.repeat(jnp.exp(draws), shape[position] // blocks).reshape((-1,) + (1,) * (len(shape) - position - 1))

    loudness = one(*shards[0])
    for cut in shards[1:]:
        loudness = loudness * one(*cut)
    return loudness


def scatter_about(stream_key, dims, width, most, cuts=(), kind=jnp.bfloat16):
    drawn = width * jax.random.normal(stream_key, dims, jnp.float32)
    if cuts:
        drawn = drawn * level_of(stream_key, dims, cuts, -0.22, 0.18)
    return jnp.clip(drawn, -most, most).astype(kind)


def setup_inputs(seed: int = 0) -> dict:
    key_list = jax.random.split(jax.random.key(seed), 6)
    features = scatter_about(key_list[0], (NX, NY, NZ, C_IN), 1.0, 6.0, ((0, 8), (1, 16)))
    occupancy = with_ends((jax.random.randint(key_list[1], (NX, NY, NZ), 0, 2) < 1).astype(jnp.int32), jax.random.fold_in(key_list[1], 1), 0, 1)
    weight = scatter_about(key_list[2], (KV, C_IN, C_OUT), (KV * C_IN) ** -0.5, 0.109375)
    owner = draw_owner(jax.random.fold_in(key_list[5], 71), 0)
    cotangent = scatter_about(key_list[4], (N_GX, N_GY, N_GY * CAP, 64 * C_OUT), 1.0, 6.0, ((0, 8), (1, 16)))
    return dict(features=features, occupancy=occupancy, weight=weight, owner=owner, cotangent=cotangent)


def offset_list():
    return [(step_x, step_y, step_z) for step_x in range(3) for step_y in range(3) for step_z in range(3)]


def reference(features, occupancy, weight, owner, cotangent):
    half_x, half_y, half_z = NX // 2, NY // 2, NZ // 2
    bricks_x, bricks_y, bricks_z = SX // 8, SY // 8, SZ // 8
    occupied = occupancy.astype(features.dtype)
    masked = features * occupied[..., None]
    padded = jnp.pad(masked, ((1, 0), (1, 0), (1, 0), (0, 0)))
    active = occupancy.reshape(half_x, 2, half_y, 2, half_z, 2).max(axis=(1, 3, 5))
    total = jnp.zeros((half_x * half_y * half_z, C_OUT), jnp.float32)
    for index, (step_x, step_y, step_z) in enumerate(offset_list()):
        piece = padded[step_x:step_x + NX:2, step_y:step_y + NY:2, step_z:step_z + NZ:2].reshape(-1, C_IN)
        total = total + jnp.dot(piece, weight[index], preferred_element_type=jnp.float32)
    total = total.reshape(half_x, half_y, half_z, C_OUT)
    output = (total * active.astype(jnp.float32)[..., None]).astype(jnp.bfloat16)
    bricks = output.reshape(N_GX, bricks_x, 4, N_GY, bricks_y, 4, bricks_z, 4, C_OUT)
    bricks = bricks.transpose(0, 3, 1, 4, 6, 2, 5, 7, 8).reshape(N_GX, N_GY, BRICKS_DEV, 64 * C_OUT)
    onehot = (owner[..., None] == jnp.arange(N_GY, dtype=jnp.int32)).astype(jnp.int32)
    ranks = jnp.sum((jnp.cumsum(onehot, axis=2) - onehot) * onehot, axis=3)
    sources = jnp.arange(N_GY, dtype=jnp.int32)[None, :, None]
    flat_slot = (owner * (N_GY * CAP) + sources * CAP + ranks).astype(jnp.int32)
    rows_x = jnp.arange(N_GX, dtype=jnp.int32)[:, None, None]
    owned = jnp.zeros((N_GX, N_GY * N_GY * CAP, 64 * C_OUT), jnp.bfloat16)
    owned = owned.at[rows_x, flat_slot].set(bricks)
    owned_output = owned.reshape(N_GX, N_GY, N_GY * CAP, 64 * C_OUT)
    back = cotangent.reshape(N_GX, N_GY * N_GY * CAP, 64 * C_OUT)[rows_x, flat_slot]
    back = back.reshape(N_GX, N_GY, bricks_x, bricks_y, bricks_z, 4, 4, 4, C_OUT)
    back = back.transpose(0, 2, 5, 1, 3, 6, 4, 7, 8).reshape(half_x, half_y, half_z, C_OUT)
    upstream = back * active.astype(jnp.bfloat16)[..., None]
    upstream_flat = upstream.reshape(-1, C_OUT)
    scale = float(half_x * half_y * half_z) ** -0.5
    grads = []
    grid = jnp.zeros((NX + 1, NY + 1, NZ + 1, C_IN), jnp.float32)
    for index, (step_x, step_y, step_z) in enumerate(offset_list()):
        piece = padded[step_x:step_x + NX:2, step_y:step_y + NY:2, step_z:step_z + NZ:2].reshape(-1, C_IN)
        grads.append(jnp.dot(piece.T, upstream_flat, preferred_element_type=jnp.float32))
        spread = jnp.dot(upstream_flat, weight[index].T, preferred_element_type=jnp.float32)
        grid = grid.at[step_x:step_x + NX:2, step_y:step_y + NY:2, step_z:step_z + NZ:2].add(spread.reshape(half_x, half_y, half_z, C_IN))
    grad_weight = jnp.stack(grads, 0) * scale
    grad_input = (grid[1:, 1:, 1:] * occupancy.astype(jnp.float32)[..., None]).astype(jnp.bfloat16)
    return (owned_output, grad_input, grad_weight)
```

```python
import jax
import jax.numpy as jnp
from jax import lax
from jax.experimental import pallas as pl
from jax.experimental.pallas import tpu as pltpu
from jax.sharding import PartitionSpec as P

BF = jnp.bfloat16
F32 = jnp.float32
MESH = pl.DeviceIdType.MESH
TAPS = 27
TILES = 54


def iota2(shape, dim):
    return lax.broadcasted_iota(jnp.int32, shape, dim)


def as_bf(cond):
    return jnp.where(cond, 1.0, 0.0).astype(F32).astype(BF)


def dot(a, b):
    return jnp.dot(a, b, preferred_element_type=F32)


def dot_nt(a, b):
    return lax.dot_general(a, b, (((1,), (1,)), ((), ())), preferred_element_type=F32)


def row_coords(rows):
    return rows // 128, (rows // 16) % 8, (rows // 4) % 4, rows % 4


def kernel(
    n_gx, n_gy, cap, per,
    slot_ref, inv_ref, occ_ref, feat, weight, cot,
    owned_out, gin_out, gw_out,
    fp, pt, mk, act, bk, cv, csend, ret, outg, arr, wv, ub, yhu, ysu, uu, upt,
    xs, ys, gi, dwf, s1s, s1r, s2s, s2r, s3s, s3r, ag, gws, pk, pc, po, qs, pysel,
    sem_feat, sem_in, sem_loc, sem_out, sem_gi, sem_gw,
    a1_s, a1_r, a2_s, a2_r, h_s, h_r, u_s, u_r,
    r1_s, r1_r, r2_s, r2_r, r3_s, r3_r, g4_s, g4_r, g5_s, g5_r, g6_s, g6_r,
):
    n_x = n_gx // 2
    i = lax.axis_index("gx")
    j = lax.axis_index("gy")
    xq = i // 2
    core = lax.rem(i, 2)
    sib = 2 * xq + 1 - core
    nxt_i, prv_i = lax.rem(i + 1, n_gx), lax.rem(i + n_gx - 1, n_gx)
    nxt_j, prv_j = lax.rem(j + 1, n_gy), lax.rem(j + n_gy - 1, n_gy)

    cot_copy = pltpu.make_async_copy(cot.at[0, 0], cv, sem_in.at[0])
    cot_copy.start()

    def feat_copy(x):
        return pltpu.make_async_copy(feat.at[x], fp.at[x + 1, pl.ds(1, 16)], sem_feat.at[x])

    for x in range(15, -1, -1):
        feat_copy(x).start()
    w_copy = pltpu.make_async_copy(weight, wv, sem_in.at[1])
    w_copy.start()

    barrier = pltpu.get_barrier_semaphore()
    peers = [(i, lax.rem(j + d, n_gy)) for d in range(1, n_gy)]
    peers += [(lax.rem(i + d, n_gx), j) for d in range(2, n_gx - 1, 2)]
    peers += [(nxt_i, j), (prv_i, j), (nxt_i, nxt_j), (prv_i, prv_j)]
    for peer in peers:
        pl.semaphore_signal(barrier, inc=1, device_id=peer, device_id_type=MESH)

    r, c = iota2((128, 256), 0), iota2((128, 256), 1)
    _, bz, vy, vz = row_coords(r)
    oz = 4 * bz + vz
    for kz in range(3):
        pk[kz] = as_bf((vy == c // 64) & (2 * oz + kz - 1 == c % 64))
    pk[3] = as_bf((vy == c // 64) & (oz == (c % 64) // 2))
    r, c = iota2((256, 256), 0), iota2((256, 256), 1)
    pc[0] = as_bf((r // 16 == c % 16) & (r % 16 == c // 16))
    pc[1] = as_bf(r == c)
    _, cbz, cvy, cvz = row_coords(c % 128)
    po[...] = as_bf((cvy == r // 64) & (8 * cbz + 2 * cvz + c // 128 == r % 64))
    rby, rbz, rvy, rvz = row_coords(r)
    cby, cbz, cvy, cvz = row_coords(c)
    roz, coz = 4 * rbz + rvz, 4 * cbz + cvz
    roy, coy = 4 * rby + rvy, 4 * cby + cvy
    qs[0] = as_bf((roy == coy) & (roz + 1 == coz))
    qs[1] = as_bf((roy + 1 == coy) & (roz == coz))
    qs[2] = as_bf((roy + 1 == coy) & (roz + 1 == coz))
    r, c = iota2((256, 128), 0), iota2((256, 128), 1)
    rby, rbz, rvy, rvz = row_coords(r)
    top = (4 * rby + rvy == 7) & (c < 32)
    qs[3, :, 0:128] = as_bf(top & (4 * rbz + rvz == c))
    qs[3, :, 128:256] = as_bf(top & (4 * rbz + rvz + 1 == c))
    r, c = iota2((128, 128), 0), iota2((128, 128), 1)
    _, cbz, cvy, cvz = row_coords(c)
    pysel[...] = as_bf((r < 32) & (cvy == 0) & (4 * cbz + cvz == r))

    pl.semaphore_wait(barrier, len(peers))

    cot_copy.wait()

    def cot_step(n, carry):
        t, vg = n // 4, n % 4
        rhs = jnp.concatenate(
            [
                cv[pl.ds(pl.multiple_of(16 * t, 16), 16), pl.ds(pl.multiple_of(4096 * vg + 256 * v, 256), 256)]
                for v in range(16)
            ],
            0,
        )
        res = dot(pc[0], rhs).astype(BF).reshape(16, 16, 256)
        csend[pl.ds(16 * t, 16), pl.ds(pl.multiple_of(16 * vg, 16), 16), :] = res
        return carry

    lax.fori_loop(0, 12, cot_step, 0)

    def a2a(d, src, dst, s_sem, r_sem):
        to = lax.rem(j + d, n_gy)
        return pltpu.make_async_remote_copy(
            src_ref=src.at[pl.ds(to * cap, cap)],
            dst_ref=dst.at[pl.ds(j * cap, cap)],
            send_sem=s_sem.at[d],
            recv_sem=r_sem.at[d],
            device_id=(i, to),
            device_id_type=MESH,
        )

    def a2a_arrival(d, src, dst, s_sem, r_sem):
        frm = lax.rem(j - d + n_gy, n_gy)
        return pltpu.make_async_remote_copy(
            src_ref=src.at[pl.ds(frm * cap, cap)],
            dst_ref=dst.at[pl.ds(frm * cap, cap)],
            send_sem=s_sem.at[d],
            recv_sem=r_sem.at[d],
            device_id=(i, frm),
            device_id_type=MESH,
        )

    for d in range(1, n_gy):
        a2a(d, csend, ret, a1_s, a1_r).start()
    own1 = pltpu.make_async_copy(
        csend.at[pl.ds(j * cap, cap)], ret.at[pl.ds(j * cap, cap)], sem_loc.at[0]
    )
    own1.start()

    def occ_row(x, y):
        return occ_ref[x, pl.ds(y, 1), :].astype(F32)

    def lanes_of(rows):
        return jnp.concatenate(rows, 1)

    def wide(row):
        return jnp.broadcast_to(row, (16, 256)).astype(BF)

    def masked_rows(mat, row):
        rows = mat.shape[0]
        m = wide(row)
        return (mat.reshape(rows // 16, 16, 256) * m[None]).reshape(rows, 256)

    feat_copy(15).wait()
    for by in range(2):
        for py in range(2):
            row = lanes_of([occ_row(15, 8 * by + 2 * v + py) for v in range(4)])
            rhs = jnp.concatenate([fp[16, 1 + 8 * by + 2 * v + py] for v in range(4)], 0)
            res = dot(masked_rows(pc[1], row), rhs).astype(BF)
            for v in range(4):
                xs[8 * by + 2 * v + py] = res[64 * v : 64 * v + 64]

    def remote(src, dst, s_sem, r_sem, to):
        return pltpu.make_async_remote_copy(
            src_ref=src, dst_ref=dst, send_sem=s_sem, recv_sem=r_sem,
            device_id=to, device_id_type=MESH,
        )

    halo_x = remote(xs, fp.at[0, pl.ds(1, 16)], h_s.at[0], h_r.at[0], (nxt_i, j))
    halo_x.start()
    for x in range(14, -1, -1):
        feat_copy(x).wait()

    def mask_y(x, carry):
        row = lanes_of([occ_row(x, 9 + 2 * v) for v in range(4)])
        rhs = jnp.concatenate([fp[x + 1, 10 + 2 * v] for v in range(4)], 0)
        ys[x] = dot(masked_rows(pc[1, 192:256, :], row), rhs).astype(BF)
        return carry

    lax.fori_loop(0, 16, mask_y, 0)
    halo_y = remote(ys, fp.at[pl.ds(1, 16), 0], h_s.at[1], h_r.at[1], (i, nxt_j))
    halo_y.start()
    halo_c = remote(ys.at[15], fp.at[0, 0], h_s.at[2], h_r.at[2], (nxt_i, nxt_j))
    halo_c.start()

    ones = jnp.ones((256, 128), F32).astype(BF)

    def prep(xp, by, ky, row, own):
        rhs = jnp.concatenate([fp[xp, 8 * by + 2 * v + ky] for v in range(4)], 0)
        with_mask = own and ky > 0
        if with_mask:
            rhs = jnp.concatenate([rhs, ones], 1)
        for kz in range(3):
            res = dot(masked_rows(pk[kz], row), rhs if kz > 0 or not with_mask else rhs[:, :128])
            col = (3 * ky + kz) * 128
            pt[xp, by * 128 : by * 128 + 128, col : col + 128] = res[:, :128].astype(BF)
            if with_mask and kz > 0:
                mk[xp - 1, 2 * (ky - 1) + kz - 1, by * 128 : by * 128 + 128, :] = res[:, 128:].astype(BF)

    def prep_own(x, carry):
        for by, ky in ((0, 1), (0, 2), (1, 0), (1, 1), (1, 2)):
            row = lanes_of([occ_row(x, 8 * by + 2 * v + ky - 1) for v in range(4)])
            prep(x + 1, by, ky, row, True)
        return carry

    lax.fori_loop(0, 16, prep_own, 0)

    def count_active(ox, carry):
        for by in range(2):
            total = jnp.zeros((1, 256), F32)
            for px in range(2):
                for py in range(2):
                    total = total + lanes_of([occ_row(2 * ox + px, 8 * by + 2 * v + py) for v in range(4)])
            count = dot(masked_rows(pk[3], total), ones)
            act[ox, by * 128 : by * 128 + 128, :] = jnp.where(count > 0.5, 1.0, 0.0).astype(BF)
        return carry

    lax.fori_loop(0, 8, count_active, 0)

    ok_x = jnp.where(i > 0, 1.0, 0.0).astype(F32)
    ok_y = jnp.where(j > 0, 1.0, 0.0).astype(F32)
    halo_x.wait()
    halo_y.wait()
    halo_c.wait()

    def prep_halo_y(x, carry):
        row = lanes_of([jnp.full((1, 64), ok_y, F32)] + [occ_row(x, 2 * v + 1) for v in range(3)])
        prep(x + 1, 0, 0, row, False)
        return carry

    lax.fori_loop(0, 16, prep_halo_y, 0)
    row_x = jnp.full((1, 256), ok_x, F32)
    corner = jnp.where(iota2((1, 256), 1) < 64, ok_x * ok_y, ok_x)
    for by in range(2):
        for ky in range(3):
            prep(0, by, ky, corner if (by == 0 and ky == 0) else row_x, False)

    w_copy.wait()

    def forward(ox, carry):
        lhs = jnp.concatenate([pt[2 * ox], pt[2 * ox + 1], pt[2 * ox + 2]], 1)
        acc = dot(lhs, wv[...])
        a = act[ox]
        a = jnp.concatenate([a, a], 1).astype(F32)
        bk[pl.ds(ox * 16, 16)] = (acc * a).astype(BF).reshape(16, 16, 256)
        return carry

    lax.fori_loop(0, 8, forward, 0)

    def pack(s, carry):
        base = inv_ref[s]
        keep = jnp.where(base >= 0, 1.0, 0.0).astype(F32)
        at = jnp.maximum(base, 0)
        flag = jnp.full((16, 256), keep, F32).astype(BF)
        for vx in range(4):
            outg[s, vx * 16 : vx * 16 + 16, :] = bk[at + 16 * vx] * flag
        return carry

    lax.fori_loop(0, n_gy * cap, pack, 0)

    own1.wait()
    for d in range(1, n_gy):
        a2a_arrival(d, csend, ret, a1_s, a1_r).wait_recv()
    for d in range(1, n_gy):
        a2a(d, outg, arr, a2_s, a2_r).start()
    own2 = pltpu.make_async_copy(
        outg.at[pl.ds(j * cap, cap)], arr.at[pl.ds(j * cap, cap)], sem_loc.at[1]
    )
    own2.start()

    def place(b, carry):
        s = slot_ref[b]
        bx, rest = b // 16, b % 16
        for vx in range(4):
            off = pl.multiple_of(rest * 16, 16)
            a = act[bx * 4 + vx, pl.ds(off, 16), :]
            a = jnp.concatenate([a, a], 1)
            ub[bx * 4 + vx, pl.ds(off, 16), :] = ret[s, vx * 16 : vx * 16 + 16, :] * a
        return carry

    lax.fori_loop(0, 32, place, 0)

    for ox in range(8):
        ysu[ox] = dot(pysel[...], ub[ox, 0:128, :])[0:32].astype(BF)
    up_x = remote(ub.at[0], ub.at[8], u_s.at[0], u_r.at[0], (prv_i, j))
    up_y = remote(ysu, yhu.at[pl.ds(0, 8)], u_s.at[1], u_r.at[1], (i, prv_j))
    up_c = remote(ysu.at[0], yhu.at[8], u_s.at[2], u_r.at[2], (prv_i, prv_j))
    up_x.start()
    up_y.start()
    up_c.start()

    for ox in range(8):
        upt[:, ox * 256 : ox * 256 + 256] = dot_nt(pc[1], ub[ox]).astype(BF)

    mine = pl.multiple_of(core * 128, 128)
    other = pl.multiple_of(128 - core * 128, 128)

    def stage1(kx):
        cols = pl.ds(kx * 1152, 1152)
        return remote(s1s.at[:, cols], s1r.at[:, cols], r1_s.at[kx], r1_r.at[kx], (sib, j))

    for kx in range(3):
        for n in range(5):
            width = 256 if n < 4 else 128
            rhs = jnp.concatenate(
                [pt[2 * ox + kx, :, n * 256 : n * 256 + width] for ox in range(8)], 0
            )
            col = kx * 1152 + n * 256
            dwf[:, col : col + width] = dot(upt[...], rhs)
        s1s[:, kx * 1152 : kx * 1152 + 1152] = dwf[pl.ds(other, 128), kx * 1152 : kx * 1152 + 1152].astype(BF)
        stage1(kx).start()

    up_x.wait()
    up_y.wait()
    up_c.wait()
    okn_x = jnp.where(i < n_gx - 1, 1.0, 0.0).astype(F32)
    okn_y = jnp.where(j < n_gy - 1, 1.0, 0.0).astype(F32)

    def shifts(ox, carry):
        last = jnp.where(ox == 8, okn_x, 1.0).astype(F32)
        base = (ub[ox].astype(F32) * last).astype(BF)
        halo = (yhu[ox].astype(F32) * (last * okn_y)).astype(BF)
        halo = jnp.concatenate([halo, jnp.zeros((96, 256), BF)], 0)
        uu[0, ox, :, 0:256] = base
        uu[0, ox, :, 256:512] = dot(qs[0], base).astype(BF)
        uu[1, ox, :, 0:256] = (dot(qs[1], base) + dot(qs[3, :, 0:128], halo)).astype(BF)
        uu[1, ox, :, 256:512] = (dot(qs[2], base) + dot(qs[3, :, 128:256], halo)).astype(BF)
        return carry

    lax.fori_loop(0, 9, shifts, 0)

    lists = (((1, 0),), ((2, 0), (0, 1)))

    def gin_copy(x):
        return pltpu.make_async_copy(gi.at[x], gin_out.at[x], sem_gi.at[x])

    def grad_in(ox, carry):
        for px in range(2):
            for py in range(2):
                both, odd = None, None
                for a, sx in lists[px]:
                    for b, sy in lists[py]:
                        k = 9 * a + 3 * b
                        one = dot_nt(uu[sy, ox + sx, :, 0:256], wv[(k + 1) * 128 : (k + 3) * 128, :])
                        two = dot_nt(uu[sy, ox + sx, :, 256:512], wv[k * 128 : (k + 1) * 128, :])
                        both = one if both is None else both + one
                        odd = two if odd is None else odd + two
                m0 = mk[2 * ox + px, 2 * py].astype(F32)
                m1 = mk[2 * ox + px, 2 * py + 1].astype(F32)
                g0 = (both[:, :128] * m0).astype(BF)
                g1 = ((both[:, 128:] + odd) * m1).astype(BF)
                rhs = jnp.concatenate(
                    [
                        jnp.concatenate([g0[:128], g1[:128]], 0),
                        jnp.concatenate([g0[128:], g1[128:]], 0),
                    ],
                    1,
                )
                res = dot(po[...], rhs).astype(BF)
                for by in range(2):
                    for v in range(4):
                        gi[2 * ox + px, 8 * by + 2 * v + py] = res[64 * v : 64 * v + 64, 128 * by : 128 * by + 128]
            gin_copy(2 * ox + px).start()
        return carry

    lax.fori_loop(0, 2, grad_in, 0)

    def stage2(d):
        to = lax.rem(xq + d, n_x)
        return remote(s2s.at[to], s2r.at[xq], r2_s.at[d], r2_r.at[d], (2 * to + core, j))

    def stage2_arrival(d):
        frm = lax.rem(xq - d + n_x, n_x)
        return remote(s2s.at[frm], s2r.at[frm], r2_s.at[d], r2_r.at[d], (2 * frm + core, j))

    for kx in range(3):
        stage1(kx).wait()

    def sum1(q, carry):
        at = pl.multiple_of(mine + q * s2s.shape[1], 16)
        rows = s2s.shape[1]
        mid = dwf[pl.ds(at, rows), :] + s1r[pl.ds(pl.multiple_of(q * rows, 16), rows), :].astype(F32)
        dwf[pl.ds(at, rows), :] = mid
        s2s[q] = mid.astype(BF)
        return carry

    lax.fori_loop(0, n_x, sum1, 0)
    for d in range(1, n_x):
        stage2(d).start()

    lax.fori_loop(2, 6, grad_in, 0)

    for d in range(1, n_x):
        stage2_arrival(d).wait_recv()
    rows2 = s2s.shape[1]
    for half in range(rows2 // 16):
        at = pl.multiple_of(mine + xq * rows2 + half * 16, 16)
        total = dwf[pl.ds(at, 16), :]
        for d in range(1, n_x):
            frm = lax.rem(xq + d, n_x)
            total = total + s2r[frm, half * 16 : half * 16 + 16, :].astype(F32)
        total = total.astype(BF)
        for tap in range(TAPS):
            s3s[half * TAPS + tap] = total[:, tap * 128 : tap * 128 + 128]
    used = (rows2 // 16) * TAPS
    for t in range(used, n_gy * per):
        s3s[t] = jnp.zeros((16, 128), BF)

    def stage3(d):
        to = lax.rem(j + d, n_gy)
        return remote(s3s.at[pl.ds(to * per, per)], s3r.at[j], r3_s.at[d], r3_r.at[d], (i, to))

    def stage3_arrival(d):
        frm = lax.rem(j - d + n_gy, n_gy)
        return remote(s3s.at[pl.ds(frm * per, per)], s3r.at[frm], r3_s.at[d], r3_r.at[d], (i, frm))

    for d in range(1, n_gy):
        stage3(d).start()

    lax.fori_loop(6, 8, grad_in, 0)

    for d in range(1, n_gy):
        stage3_arrival(d).wait_recv()
    total = s3s[pl.ds(j * per, per)].astype(F32)
    for d in range(1, n_gy):
        total = total + s3r[lax.rem(j + d, n_gy)].astype(F32)
    ag[core, xq, pl.ds(j * per, per)] = total.astype(BF)

    def stage4(d):
        to = lax.rem(j + d, n_gy)
        here = ag.at[core, xq, pl.ds(j * per, per)]
        return remote(here, here, g4_s.at[d], g4_r.at[d], (i, to))

    def stage4_arrival(d):
        frm = lax.rem(j - d + n_gy, n_gy)
        here = ag.at[core, xq, pl.ds(frm * per, per)]
        return remote(here, here, g4_s.at[d], g4_r.at[d], (i, frm))

    for d in range(1, n_gy):
        stage4(d).start()

    own2.wait()
    for d in range(1, n_gy):
        a2a_arrival(d, outg, arr, a2_s, a2_r).wait_recv()
    for d in range(1, n_gy):
        a2a(d, csend, ret, a1_s, a1_r).wait_send()

    def owned_step(n, carry):
        t, vg = n // 4, n % 4
        rhs = arr[pl.ds(16 * t, 16), pl.ds(pl.multiple_of(16 * vg, 16), 16), :].reshape(256, 256)
        res = dot(pc[0], rhs).astype(BF)
        for v in range(16):
            cv[pl.ds(pl.multiple_of(16 * t, 16), 16), pl.ds(pl.multiple_of(4096 * vg + 256 * v, 256), 256)] = res[16 * v : 16 * v + 16]
        return carry

    lax.fori_loop(0, 12, owned_step, 0)
    owned_copy = pltpu.make_async_copy(cv, owned_out.at[0, 0], sem_out.at[0])
    owned_copy.start()

    for d in range(1, n_gy):
        stage4_arrival(d).wait_recv()

    def stage5(d):
        to = lax.rem(xq + d, n_x)
        here = ag.at[core, xq]
        return remote(here, here, g5_s.at[d], g5_r.at[d], (2 * to + core, j))

    def stage5_arrival(d):
        frm = lax.rem(xq - d + n_x, n_x)
        here = ag.at[core, frm]
        return remote(here, here, g5_s.at[d], g5_r.at[d], (2 * frm + core, j))

    def stage6(d):
        frm = lax.rem(xq - d + n_x, n_x)
        here = ag.at[core, frm]
        return remote(here, here, g6_s.at[d], g6_r.at[d], (sib, j))

    def stage6_arrival(d):
        frm = lax.rem(xq - d + n_x, n_x)
        here = ag.at[1 - core, frm]
        return remote(here, here, g6_s.at[d], g6_r.at[d], (sib, j))

    for d in range(1, n_x):
        stage5(d).start()
    stage6(0).start()
    for d in range(1, n_x):
        stage5_arrival(d).wait_recv()
        stage6(d).start()
    for d in range(n_x):
        stage6_arrival(d).wait_recv()

    scale = float(8 * 8 * 32 * n_gx * n_gy) ** -0.5

    def gw_copy(tap):
        return pltpu.make_async_copy(gws.at[tap], gw_out.at[tap], sem_gw.at[tap])

    def finish(tap, carry):
        rows = jnp.concatenate(
            [
                ag[cc, q, half * TAPS + tap]
                for cc in range(2)
                for q in range(n_x)
                for half in range(rows2 // 16)
            ],
            0,
        )
        gws[tap] = dot_nt(pc[1, 0:128, 0:128], rows) * scale
        gw_copy(tap).start()
        return carry

    lax.fori_loop(0, TAPS, finish, 0)

    for d in range(1, n_gy):
        a2a(d, outg, arr, a2_s, a2_r).wait_send()
        stage3(d).wait_send()
        stage4(d).wait_send()
    for d in range(1, n_x):
        stage2(d).wait_send()
        stage5(d).wait_send()
    for d in range(n_x):
        stage6(d).wait_send()
    owned_copy.wait()
    for x in range(16):
        gin_copy(x).wait()
    for tap in range(TAPS):
        gw_copy(tap).wait()


def on_device(n_gx, n_gy, features, occupancy, weight, owner, cotangent):
    cap = cotangent.shape[2] // n_gy
    n_x = n_gx // 2
    rows2 = 128 // n_x
    per = -(-(rows2 // 16) * TAPS // n_gy)
    slots_n = n_gy * cap
    targets = owner.reshape(-1)
    b = jnp.arange(32, dtype=jnp.int32)
    earlier = (targets[:, None] == targets[None, :]) & (b[:, None] > b[None, :])
    slots = targets * cap + jnp.sum(earlier.astype(jnp.int32), axis=1)
    base = (b // 16) * 64 + b % 16
    hit = jnp.arange(slots_n, dtype=jnp.int32)[:, None] == slots[None, :]
    inv = jnp.sum(jnp.where(hit, base[None, :] + 1, 0), axis=1) - 1

    V = pltpu.VMEM
    D = pltpu.SemaphoreType.DMA
    scratch = [
        V((17, 17, 64, 128), BF),
        V((17, 256, 1152), BF),
        V((16, 4, 256, 128), BF),
        V((8, 256, 128), BF),
        V((128, 16, 256), BF),
        V((slots_n, 16384), BF),
        V((slots_n, 64, 256), BF),
        V((slots_n, 64, 256), BF),
        V((slots_n, 64, 256), BF),
        V((slots_n, 64, 256), BF),
        V((TAPS * 128, 256), BF),
        V((9, 256, 256), BF),
        V((9, 32, 256), BF),
        V((8, 32, 256), BF),
        V((2, 9, 256, 512), BF),
        V((256, 2048), BF),
        V((16, 64, 128), BF),
        V((16, 64, 128), BF),
        V((16, 16, 64, 128), BF),
        V((256, TAPS * 128), F32),
        V((128, TAPS * 128), BF),
        V((128, TAPS * 128), BF),
        V((n_x, rows2, TAPS * 128), BF),
        V((n_x, rows2, TAPS * 128), BF),
        V((n_gy * per, 16, 128), BF),
        V((n_gy, per, 16, 128), BF),
        V((2, n_x, n_gy * per, 16, 128), BF),
        V((TAPS, 128, 256), F32),
        V((4, 128, 256), BF),
        V((2, 256, 256), BF),
        V((256, 256), BF),
        V((4, 256, 256), BF),
        V((128, 128), BF),
        D((16,)), D((2,)), D((2,)), D((1,)), D((16,)), D((TAPS,)),
        D((n_gy,)), D((n_gy,)), D((n_gy,)), D((n_gy,)),
        D((3,)), D((3,)), D((3,)), D((3,)),
        D((3,)), D((3,)), D((n_x,)), D((n_x,)),
        D((n_gy,)), D((n_gy,)), D((n_gy,)), D((n_gy,)),
        D((n_x,)), D((n_x,)), D((n_x,)), D((n_x,)),
    ]

    def body(*refs):
        kernel(n_gx, n_gy, cap, per, *refs)

    return pl.pallas_call(
        body,
        out_shape=(
            jax.ShapeDtypeStruct(cotangent.shape, BF),
            jax.ShapeDtypeStruct(features.shape, BF),
            jax.ShapeDtypeStruct(weight.shape, F32),
        ),
        in_specs=[
            pl.BlockSpec(memory_space=pltpu.SMEM),
            pl.BlockSpec(memory_space=pltpu.SMEM),
            pl.BlockSpec(memory_space=pltpu.VMEM),
            pl.BlockSpec(memory_space=pl.ANY),
            pl.BlockSpec(memory_space=pl.ANY),
            pl.BlockSpec(memory_space=pl.ANY),
        ],
        out_specs=[pl.BlockSpec(memory_space=pl.ANY)] * 3,
        scratch_shapes=scratch,
        compiler_params=pltpu.CompilerParams(
            collective_id=0, has_side_effects=True, vmem_limit_bytes=63 * 1024 * 1024
        ),
        cost_estimate=pl.CostEstimate(
            flops=12_000_000_000, bytes_accessed=20_000_000, transcendentals=0
        ),
    )(slots, inv, occupancy, features, weight.reshape(TAPS * 128, 256), cotangent)


def solution(mesh):
    n_gx, n_gy = mesh.shape["gx"], mesh.shape["gy"]

    def local(*args):
        return on_device(n_gx, n_gy, *args)

    in_specs = (
        P("gx", "gy", None, None),
        P("gx", "gy", None),
        P(),
        P("gx", "gy", None),
        P("gx", "gy", None, None),
    )
    out_specs = (P("gx", "gy", None, None), P("gx", "gy", None, None), P())
    return jax.shard_map(
        local, mesh=mesh, in_specs=in_specs, out_specs=out_specs, check_vma=False
    )
```

```python
import jax
import jax.numpy as jnp
from jax import lax
from jax.experimental import pallas as pl
from jax.experimental.pallas import tpu as pltpu
from jax.sharding import PartitionSpec as P

BF = jnp.bfloat16
F32 = jnp.float32
MESH = pl.DeviceIdType.MESH
TAPS = 27
CHUNKS = ((0, 8), (8, 16), (16, 27))
FAR_FIRST = (10, 6, 9, 11, 14, 5, 7, 13, 15, 2, 8, 1, 3, 4, 12)


def iota2(shape, dim):
    return lax.broadcasted_iota(jnp.int32, shape, dim)


def as_bf(cond):
    return jnp.where(cond, 1.0, 0.0).astype(F32).astype(BF)


def dot(a, b):
    return jnp.dot(a, b, preferred_element_type=F32)


def dot_nt(a, b):
    return lax.dot_general(a, b, (((1,), (1,)), ((), ())), preferred_element_type=F32)


def chunk_plan(n_x, n_gy):
    halves = 128 // n_x // 16
    plan, first, mine = [], 0, 0
    for t0, t1 in CHUNKS:
        used = halves * (t1 - t0)
        per = -(-used // n_gy)
        plan.append((used, per, first, mine))
        first += per * n_gy
        mine += per
    return plan, first, mine


def tile_of(plan, half, tap):
    for (t0, t1), (_, _, first, _) in zip(CHUNKS, plan):
        if t0 <= tap < t1:
            return first + half * (t1 - t0) + tap - t0


def partner(j, d):
    total, bit = 0, 1
    while bit <= 8:
        b = (j // bit) % 2
        total = total + bit * (1 - b if d & bit else b)
        bit *= 2
    return total


def row_coords(rows):
    return rows // 128, (rows // 16) % 8, (rows // 4) % 4, rows % 4


def kernel(
    n_gx, n_gy, cap,
    slot_ref, inv_ref, occ_ref, feat, weight, cot,
    ov, gi, ag,
    fp, pt, mk, act, bk, cv, csend, ret, outg, arr, wv, ub, yhu, ysu, uu, upt,
    xs, ys, dwf, s1s, s1r, s2s, s2r, s3s, s3r, pk, pc, po, qs, pysel,
    sem_feat, sem_in, sem_loc,
    a1_s, a1_r, a2_s, a2_r, h_s, h_r, u_s, u_r,
    r1_s, r1_r, r2_s, r2_r, r3_s, r3_r, g4_s, g4_r, g5_s, g5_r, g6_s, g6_r,
):
    n_x = n_gx // 2
    i = lax.axis_index("gx")
    j = lax.axis_index("gy")
    xq = i // 2
    core = lax.rem(i, 2)
    sib = 2 * xq + 1 - core
    nxt_i, prv_i = lax.rem(i + 1, n_gx), lax.rem(i + n_gx - 1, n_gx)
    nxt_j, prv_j = lax.rem(j + 1, n_gy), lax.rem(j + n_gy - 1, n_gy)

    cot_copy = pltpu.make_async_copy(cot.at[0, 0], cv, sem_in.at[0])
    cot_copy.start()

    def feat_copy(x):
        return pltpu.make_async_copy(feat.at[x], fp.at[x + 1, pl.ds(1, 16)], sem_feat.at[x])

    for x in range(15, -1, -1):
        feat_copy(x).start()
    w_copy = pltpu.make_async_copy(weight, wv, sem_in.at[1])
    w_copy.start()

    barrier = pltpu.get_barrier_semaphore()
    order = [d for d in FAR_FIRST if d < n_gy]
    peer_j = {d: partner(j, d) for d in order}
    peers = [(i, peer_j[d]) for d in order]
    peers += [(lax.rem(i + d, n_gx), j) for d in range(2, n_gx - 1, 2)]
    peers += [(nxt_i, j), (prv_i, j), (nxt_i, nxt_j), (prv_i, prv_j)]
    for peer in peers:
        pl.semaphore_signal(barrier, inc=1, device_id=peer, device_id_type=MESH)

    r, c = iota2((128, 256), 0), iota2((128, 256), 1)
    _, bz, vy, vz = row_coords(r)
    oz = 4 * bz + vz
    for kz in range(3):
        pk[kz] = as_bf((vy == c // 64) & (2 * oz + kz - 1 == c % 64))
    pk[3] = as_bf((vy == c // 64) & (oz == (c % 64) // 2))
    r, c = iota2((256, 256), 0), iota2((256, 256), 1)
    pc[0] = as_bf((r // 16 == c % 16) & (r % 16 == c // 16))
    pc[1] = as_bf(r == c)
    _, cbz, cvy, cvz = row_coords(c % 128)
    po[...] = as_bf((cvy == r // 64) & (8 * cbz + 2 * cvz + c // 128 == r % 64))
    rby, rbz, rvy, rvz = row_coords(r)
    cby, cbz, cvy, cvz = row_coords(c)
    roz, coz = 4 * rbz + rvz, 4 * cbz + cvz
    roy, coy = 4 * rby + rvy, 4 * cby + cvy
    qs[0] = as_bf((roy == coy) & (roz + 1 == coz))
    qs[1] = as_bf((roy + 1 == coy) & (roz == coz))
    qs[2] = as_bf((roy + 1 == coy) & (roz + 1 == coz))
    r, c = iota2((256, 128), 0), iota2((256, 128), 1)
    rby, rbz, rvy, rvz = row_coords(r)
    top = (4 * rby + rvy == 7) & (c < 32)
    qs[3, :, 0:128] = as_bf(top & (4 * rbz + rvz == c))
    qs[3, :, 128:256] = as_bf(top & (4 * rbz + rvz + 1 == c))
    r, c = iota2((128, 128), 0), iota2((128, 128), 1)
    _, cbz, cvy, cvz = row_coords(c)
    pysel[...] = as_bf((r < 32) & (cvy == 0) & (4 * cbz + cvz == r))

    cot_copy.wait()

    def cot_step(n, carry):
        t, vg = n // 4, n % 4
        rhs = jnp.concatenate(
            [
                cv[pl.ds(pl.multiple_of(16 * t, 16), 16), pl.ds(pl.multiple_of(4096 * vg + 256 * v, 256), 256)]
                for v in range(16)
            ],
            0,
        )
        res = dot(pc[0], rhs).astype(BF).reshape(16, 16, 256)
        csend[pl.ds(16 * t, 16), pl.ds(pl.multiple_of(16 * vg, 16), 16), :] = res
        return carry

    lax.fori_loop(0, 12, cot_step, 0)

    def remote(src, dst, s_sem, r_sem, to):
        return pltpu.make_async_remote_copy(
            src_ref=src, dst_ref=dst, send_sem=s_sem, recv_sem=r_sem,
            device_id=to, device_id_type=MESH,
        )

    def a2a(d, src, dst, s_sem, r_sem):
        to = peer_j[d]
        return remote(
            src.at[pl.ds(to * cap, cap)], dst.at[pl.ds(j * cap, cap)], s_sem.at[d], r_sem.at[d], (i, to)
        )

    def a2a_arrival(d, src, dst, s_sem, r_sem):
        frm = peer_j[d]
        here = pl.ds(frm * cap, cap)
        return remote(src.at[here], dst.at[here], s_sem.at[d], r_sem.at[d], (i, frm))

    def occ_row(x, y):
        return occ_ref[x, pl.ds(y, 1), :].astype(F32)

    def lanes_of(rows):
        return jnp.concatenate(rows, 1)

    def wide(row):
        return jnp.broadcast_to(row, (16, 256)).astype(BF)

    def masked_rows(mat, row):
        rows = mat.shape[0]
        m = wide(row)
        return (mat.reshape(rows // 16, 16, 256) * m[None]).reshape(rows, 256)

    feat_copy(15).wait()
    for by in range(2):
        for py in range(2):
            row = lanes_of([occ_row(15, 8 * by + 2 * v + py) for v in range(4)])
            rhs = jnp.concatenate([fp[16, 1 + 8 * by + 2 * v + py] for v in range(4)], 0)
            res = dot(masked_rows(pc[1], row), rhs).astype(BF)
            for v in range(4):
                xs[8 * by + 2 * v + py] = res[64 * v : 64 * v + 64]

    for x in range(14, -1, -1):
        feat_copy(x).wait()

    def mask_y(x, carry):
        row = lanes_of([occ_row(x, 9 + 2 * v) for v in range(4)])
        rhs = jnp.concatenate([fp[x + 1, 10 + 2 * v] for v in range(4)], 0)
        ys[x] = dot(masked_rows(pc[1, 192:256, :], row), rhs).astype(BF)
        return carry

    lax.fori_loop(0, 16, mask_y, 0)
    pl.semaphore_wait(barrier, len(peers))
    halo_x = remote(xs, fp.at[0, pl.ds(1, 16)], h_s.at[0], h_r.at[0], (nxt_i, j))
    halo_y = remote(ys, fp.at[pl.ds(1, 16), 0], h_s.at[1], h_r.at[1], (i, nxt_j))
    halo_c = remote(ys.at[15], fp.at[0, 0], h_s.at[2], h_r.at[2], (nxt_i, nxt_j))
    halo_y.start()
    halo_x.start()
    halo_c.start()
    for d in order:
        a2a(d, csend, ret, a1_s, a1_r).start()
    own1 = pltpu.make_async_copy(
        csend.at[pl.ds(j * cap, cap)], ret.at[pl.ds(j * cap, cap)], sem_loc.at[0]
    )
    own1.start()

    ones = jnp.ones((256, 128), F32).astype(BF)

    def prep(xp, by, ky, row, own):
        rhs = jnp.concatenate([fp[xp, 8 * by + 2 * v + ky] for v in range(4)], 0)
        with_mask = own and ky > 0
        if with_mask:
            rhs = jnp.concatenate([rhs, ones], 1)
        for kz in range(3):
            res = dot(masked_rows(pk[kz], row), rhs if kz > 0 or not with_mask else rhs[:, :128])
            col = (3 * ky + kz) * 128
            pt[xp, by * 128 : by * 128 + 128, col : col + 128] = res[:, :128].astype(BF)
            if with_mask and kz > 0:
                mk[xp - 1, 2 * (ky - 1) + kz - 1, by * 128 : by * 128 + 128, :] = res[:, 128:].astype(BF)

    def prep_own(x, carry):
        for by, ky in ((0, 1), (0, 2), (1, 0), (1, 1), (1, 2)):
            row = lanes_of([occ_row(x, 8 * by + 2 * v + ky - 1) for v in range(4)])
            prep(x + 1, by, ky, row, True)
        return carry

    lax.fori_loop(0, 16, prep_own, 0)

    def count_active(ox, carry):
        for by in range(2):
            total = jnp.zeros((1, 256), F32)
            for px in range(2):
                for py in range(2):
                    total = total + lanes_of([occ_row(2 * ox + px, 8 * by + 2 * v + py) for v in range(4)])
            count = dot(masked_rows(pk[3], total), ones)
            act[ox, by * 128 : by * 128 + 128, :] = jnp.where(count > 0.5, 1.0, 0.0).astype(BF)
        return carry

    lax.fori_loop(0, 8, count_active, 0)

    ok_x = jnp.where(i > 0, 1.0, 0.0).astype(F32)
    ok_y = jnp.where(j > 0, 1.0, 0.0).astype(F32)
    halo_x.wait()
    halo_y.wait()
    halo_c.wait()

    def prep_halo_y(x, carry):
        row = lanes_of([jnp.full((1, 64), ok_y, F32)] + [occ_row(x, 2 * v + 1) for v in range(3)])
        prep(x + 1, 0, 0, row, False)
        return carry

    lax.fori_loop(0, 16, prep_halo_y, 0)
    row_x = jnp.full((1, 256), ok_x, F32)
    corner = jnp.where(iota2((1, 256), 1) < 64, ok_x * ok_y, ok_x)
    for by in range(2):
        for ky in range(3):
            prep(0, by, ky, corner if (by == 0 and ky == 0) else row_x, False)

    w_copy.wait()

    def forward(ox, carry):
        lhs = jnp.concatenate([pt[2 * ox], pt[2 * ox + 1], pt[2 * ox + 2]], 1)
        acc = dot(lhs, wv[...])
        a = act[ox]
        a = jnp.concatenate([a, a], 1).astype(F32)
        bk[pl.ds(ox * 16, 16)] = (acc * a).astype(BF).reshape(16, 16, 256)
        return carry

    lax.fori_loop(0, 8, forward, 0)

    def pack(s, carry):
        base = inv_ref[s]
        keep = jnp.where(base >= 0, 1.0, 0.0).astype(F32)
        at = jnp.maximum(base, 0)
        flag = jnp.full((16, 256), keep, F32).astype(BF)
        for vx in range(4):
            outg[s, vx * 16 : vx * 16 + 16, :] = bk[at + 16 * vx] * flag
        return carry

    lax.fori_loop(0, n_gy * cap, pack, 0)

    own1.wait()
    for d in order:
        a2a_arrival(d, csend, ret, a1_s, a1_r).wait_recv()

    def place(b, carry):
        s = slot_ref[b]
        bx, rest = b // 16, b % 16
        for vx in range(4):
            off = pl.multiple_of(rest * 16, 16)
            a = act[bx * 4 + vx, pl.ds(off, 16), :]
            a = jnp.concatenate([a, a], 1)
            ub[bx * 4 + vx, pl.ds(off, 16), :] = ret[s, vx * 16 : vx * 16 + 16, :] * a
        return carry

    lax.fori_loop(0, 32, place, 0)

    for ox in range(8):
        ysu[ox] = dot(pysel[...], ub[ox, 0:128, :])[0:32].astype(BF)
    up_x = remote(ub.at[0], ub.at[8], u_s.at[0], u_r.at[0], (prv_i, j))
    up_y = remote(ysu, yhu.at[pl.ds(0, 8)], u_s.at[1], u_r.at[1], (i, prv_j))
    up_c = remote(ysu.at[0], yhu.at[8], u_s.at[2], u_r.at[2], (prv_i, prv_j))
    up_x.start()
    up_y.start()
    up_c.start()

    for d in order:
        a2a(d, outg, arr, a2_s, a2_r).start()
    own2 = pltpu.make_async_copy(
        outg.at[pl.ds(j * cap, cap)], arr.at[pl.ds(j * cap, cap)], sem_loc.at[1]
    )
    own2.start()

    for ox in range(8):
        upt[:, ox * 256 : ox * 256 + 256] = dot_nt(pc[1], ub[ox]).astype(BF)

    mine = pl.multiple_of(core * 128, 128)
    other = pl.multiple_of(128 - core * 128, 128)

    rows2 = 128 // n_x
    plan, _, _ = chunk_plan(n_x, n_gy)

    def columns(n):
        return slice(CHUNKS[n][0] * 128, CHUNKS[n][1] * 128)

    def tap_rows(tap):
        kx, col = tap // 9, (tap % 9) * 128
        return jnp.concatenate([pt[2 * ox + kx, :, col : col + 128] for ox in range(8)], 0)

    def stage1(n):
        cols = columns(n)
        return remote(s1s.at[:, cols], s1r.at[:, cols], r1_s.at[n], r1_r.at[n], (sib, j))

    def weight_chunk(n):
        t0, t1 = CHUNKS[n]
        for tap in range(t0, t1, 2):
            rhs = tap_rows(tap)
            if tap + 1 < t1:
                rhs = jnp.concatenate([rhs, tap_rows(tap + 1)], 1)
            dwf[:, tap * 128 : tap * 128 + rhs.shape[1]] = dot(upt[...], rhs)
        cols = columns(n)
        s1s[:, cols] = dwf[pl.ds(other, 128), cols].astype(BF)
        stage1(n).start()

    def stage2(n, d):
        cols = columns(n)
        to = lax.rem(xq + d, n_x)
        return remote(s2s.at[to, :, cols], s2r.at[xq, :, cols], r2_s.at[n, d], r2_r.at[n, d], (2 * to + core, j))

    def stage2_arrival(n, d):
        cols = columns(n)
        frm = lax.rem(xq - d + n_x, n_x)
        return remote(s2s.at[frm, :, cols], s2r.at[frm, :, cols], r2_s.at[n, d], r2_r.at[n, d], (2 * frm + core, j))

    def after1(n):
        cols = columns(n)
        stage1(n).wait()
        for q in range(n_x):
            at = pl.multiple_of(mine + q * rows2, 16)
            mid = dwf[pl.ds(at, rows2), cols] + s1r[q * rows2 : (q + 1) * rows2, cols].astype(F32)
            dwf[pl.ds(at, rows2), cols] = mid
            s2s[q, :, cols] = mid.astype(BF)
        for d in range(1, n_x):
            stage2(n, d).start()

    def stage3(n, d):
        _, per, first, own = plan[n]
        to = peer_j[d]
        return remote(
            s3s.at[pl.ds(first + to * per, per)], s3r.at[j, pl.ds(own, per)],
            r3_s.at[n, d], r3_r.at[n, d], (i, to),
        )

    def stage3_arrival(n, d):
        _, per, first, own = plan[n]
        frm = peer_j[d]
        return remote(
            s3s.at[pl.ds(first + frm * per, per)], s3r.at[frm, pl.ds(own, per)],
            r3_s.at[n, d], r3_r.at[n, d], (i, frm),
        )

    def after2(n):
        used, per, first, _ = plan[n]
        t0, t1 = CHUNKS[n]
        cols = columns(n)
        for d in range(1, n_x):
            stage2_arrival(n, d).wait_recv()
        for half in range(rows2 // 16):
            at = pl.multiple_of(mine + xq * rows2 + half * 16, 16)
            total = dwf[pl.ds(at, 16), cols]
            for d in range(1, n_x):
                frm = lax.rem(xq + d, n_x)
                total = total + s2r[frm, half * 16 : half * 16 + 16, cols].astype(F32)
            total = total.astype(BF)
            for t in range(t1 - t0):
                s3s[first + half * (t1 - t0) + t] = total[:, t * 128 : t * 128 + 128]
        for t in range(first + used, first + per * n_gy):
            s3s[t] = jnp.zeros((16, 128), BF)
        for d in order:
            stage3(n, d).start()

    def stage4(n, d):
        _, per, first, _ = plan[n]
        here = ag.at[core, xq, pl.ds(first + j * per, per)]
        return remote(here, here, g4_s.at[n, d], g4_r.at[n, d], (i, peer_j[d]))

    def stage4_arrival(n, d):
        _, per, first, _ = plan[n]
        here = ag.at[core, xq, pl.ds(first + peer_j[d] * per, per)]
        return remote(here, here, g4_s.at[n, d], g4_r.at[n, d], (i, peer_j[d]))

    def after3(n):
        _, per, first, own = plan[n]
        for d in order:
            stage3_arrival(n, d).wait_recv()
        total = s3s[pl.ds(first + j * per, per)].astype(F32)
        for d in order:
            total = total + s3r[peer_j[d], own : own + per].astype(F32)
        ag[core, xq, pl.ds(first + j * per, per)] = total.astype(BF)
        for d in order:
            stage4(n, d).start()

    def block(c, q, n):
        used, _, first, _ = plan[n]
        return ag.at[c, q, first : first + used]

    def stage5(n, d):
        to = lax.rem(xq + d, n_x)
        here = block(core, xq, n)
        return remote(here, here, g5_s.at[n, d], g5_r.at[n, d], (2 * to + core, j))

    def stage5_arrival(n, d):
        frm = lax.rem(xq - d + n_x, n_x)
        here = block(core, frm, n)
        return remote(here, here, g5_s.at[n, d], g5_r.at[n, d], (2 * frm + core, j))

    def stage6(n, d):
        here = block(core, lax.rem(xq - d + n_x, n_x), n)
        return remote(here, here, g6_s.at[n, d], g6_r.at[n, d], (sib, j))

    def stage6_arrival(n, d):
        here = block(1 - core, lax.rem(xq - d + n_x, n_x), n)
        return remote(here, here, g6_s.at[n, d], g6_r.at[n, d], (sib, j))

    def after4(n):
        for d in order:
            stage4_arrival(n, d).wait_recv()
        for d in range(1, n_x):
            stage5(n, d).start()
        stage6(n, 0).start()

    def after5(n):
        for d in range(1, n_x):
            stage5_arrival(n, d).wait_recv()
            stage6(n, d).start()

    weight_chunk(0)
    weight_chunk(1)
    after1(0)
    weight_chunk(2)
    after1(1)

    up_x.wait()
    up_y.wait()
    up_c.wait()
    okn_x = jnp.where(i < n_gx - 1, 1.0, 0.0).astype(F32)
    okn_y = jnp.where(j < n_gy - 1, 1.0, 0.0).astype(F32)

    def shifts(ox, carry):
        last = jnp.where(ox == 8, okn_x, 1.0).astype(F32)
        base = (ub[ox].astype(F32) * last).astype(BF)
        halo = (yhu[ox].astype(F32) * (last * okn_y)).astype(BF)
        halo = jnp.concatenate([halo, jnp.zeros((96, 256), BF)], 0)
        uu[0, ox, :, 0:256] = base
        uu[0, ox, :, 256:512] = dot(qs[0], base).astype(BF)
        uu[1, ox, :, 0:256] = (dot(qs[1], base) + dot(qs[3, :, 0:128], halo)).astype(BF)
        uu[1, ox, :, 256:512] = (dot(qs[2], base) + dot(qs[3, :, 128:256], halo)).astype(BF)
        return carry

    lax.fori_loop(0, 9, shifts, 0)

    lists = (((1, 0),), ((2, 0), (0, 1)))

    def grad_in(ox, carry):
        for px in range(2):
            for py in range(2):
                both, odd = None, None
                for a, sx in lists[px]:
                    for b, sy in lists[py]:
                        k = 9 * a + 3 * b
                        one = dot_nt(uu[sy, ox + sx, :, 0:256], wv[(k + 1) * 128 : (k + 3) * 128, :])
                        two = dot_nt(uu[sy, ox + sx, :, 256:512], wv[k * 128 : (k + 1) * 128, :])
                        both = one if both is None else both + one
                        odd = two if odd is None else odd + two
                m0 = mk[2 * ox + px, 2 * py].astype(F32)
                m1 = mk[2 * ox + px, 2 * py + 1].astype(F32)
                g0 = (both[:, :128] * m0).astype(BF)
                g1 = ((both[:, 128:] + odd) * m1).astype(BF)
                rhs = jnp.concatenate(
                    [
                        jnp.concatenate([g0[:128], g1[:128]], 0),
                        jnp.concatenate([g0[128:], g1[128:]], 0),
                    ],
                    1,
                )
                res = dot(po[...], rhs).astype(BF)
                for by in range(2):
                    for v in range(4):
                        gi[2 * ox + px, 8 * by + 2 * v + py] = res[64 * v : 64 * v + 64, 128 * by : 128 * by + 128]
        return carry

    def grads(lo, hi):
        lax.fori_loop(lo, hi, grad_in, 0)

    after1(2)
    grads(0, 1)
    after2(0)
    grads(1, 2)
    after2(1)
    after3(0)
    grads(2, 3)
    after2(2)
    after3(1)
    grads(3, 4)
    after4(0)
    after3(2)
    grads(4, 5)
    after4(1)
    grads(5, 6)
    after5(0)
    after4(2)
    grads(6, 8)
    after5(1)

    own2.wait()
    for d in order:
        a2a_arrival(d, outg, arr, a2_s, a2_r).wait_recv()

    def owned_step(n, carry):
        t, vg = n // 4, n % 4
        rhs = arr[pl.ds(16 * t, 16), pl.ds(pl.multiple_of(16 * vg, 16), 16), :].reshape(256, 256)
        res = dot(pc[0], rhs).astype(BF)
        for v in range(16):
            ov[pl.ds(pl.multiple_of(16 * t, 16), 16), pl.ds(pl.multiple_of(4096 * vg + 256 * v, 256), 256)] = res[16 * v : 16 * v + 16]
        return carry

    lax.fori_loop(0, 12, owned_step, 0)

    after5(2)
    for n in range(len(CHUNKS)):
        for d in range(n_x):
            stage6_arrival(n, d).wait_recv()

    for d in order:
        a2a(d, csend, ret, a1_s, a1_r).wait_send()
        a2a(d, outg, arr, a2_s, a2_r).wait_send()
    for n in range(len(CHUNKS)):
        for d in order:
            stage3(n, d).wait_send()
            stage4(n, d).wait_send()
        for d in range(1, n_x):
            stage2(n, d).wait_send()
            stage5(n, d).wait_send()
        for d in range(n_x):
            stage6(n, d).wait_send()


def finish_kernel(n_x, n_gy, scale, ov, gi, ag, owned_out, gin_out, gw_out, gws, sem_big, sem_gw):
    plan, _, _ = chunk_plan(n_x, n_gy)
    copies = [pltpu.make_async_copy(gi.at[pl.ds(4 * n, 4)], gin_out.at[pl.ds(4 * n, 4)], sem_big.at[n]) for n in range(4)]
    copies.append(pltpu.make_async_copy(ov, owned_out, sem_big.at[4]))
    for copy in copies:
        copy.start()
    eye = as_bf(iota2((128, 128), 0) == iota2((128, 128), 1))
    for tap in range(TAPS):
        rows = jnp.concatenate(
            [
                ag[c, q, tile_of(plan, half, tap)]
                for c in range(2)
                for q in range(n_x)
                for half in range(128 // n_x // 16)
            ],
            0,
        )
        gws[tap] = dot_nt(eye, rows) * scale
        copy = pltpu.make_async_copy(gws.at[tap], gw_out.at[tap], sem_gw.at[tap])
        copy.start()
        copies.append(copy)
    for copy in copies:
        copy.wait()


def on_device(n_gx, n_gy, features, occupancy, weight, owner, cotangent):
    cap = cotangent.shape[2] // n_gy
    n_x = n_gx // 2
    rows2 = 128 // n_x
    _, tiles, per = chunk_plan(n_x, n_gy)
    slots_n = n_gy * cap
    targets = owner.reshape(-1)
    b = jnp.arange(32, dtype=jnp.int32)
    earlier = (targets[:, None] == targets[None, :]) & (b[:, None] > b[None, :])
    slots = targets * cap + jnp.sum(earlier.astype(jnp.int32), axis=1)
    base = (b // 16) * 64 + b % 16
    hit = jnp.arange(slots_n, dtype=jnp.int32)[:, None] == slots[None, :]
    inv = jnp.sum(jnp.where(hit, base[None, :] + 1, 0), axis=1) - 1

    V = pltpu.VMEM
    D = pltpu.SemaphoreType.DMA
    nc = len(CHUNKS)
    scratch = [
        V((17, 17, 64, 128), BF),
        V((17, 256, 1152), BF),
        V((16, 4, 256, 128), BF),
        V((8, 256, 128), BF),
        V((128, 16, 256), BF),
        V((slots_n, 16384), BF),
        V((slots_n, 64, 256), BF),
        V((slots_n, 64, 256), BF),
        V((slots_n, 64, 256), BF),
        V((slots_n, 64, 256), BF),
        V((TAPS * 128, 256), BF),
        V((9, 256, 256), BF),
        V((9, 32, 256), BF),
        V((8, 32, 256), BF),
        V((2, 9, 256, 512), BF),
        V((256, 2048), BF),
        V((16, 64, 128), BF),
        V((16, 64, 128), BF),
        V((256, TAPS * 128), F32),
        V((128, TAPS * 128), BF),
        V((128, TAPS * 128), BF),
        V((n_x, rows2, TAPS * 128), BF),
        V((n_x, rows2, TAPS * 128), BF),
        V((tiles, 16, 128), BF),
        V((n_gy, per, 16, 128), BF),
        V((4, 128, 256), BF),
        V((2, 256, 256), BF),
        V((256, 256), BF),
        V((4, 256, 256), BF),
        V((128, 128), BF),
        D((16,)), D((2,)), D((2,)),
        D((16,)), D((16,)), D((16,)), D((16,)),
        D((3,)), D((3,)), D((3,)), D((3,)),
        D((nc,)), D((nc,)), D((nc, n_x)), D((nc, n_x)),
        D((nc, 16)), D((nc, 16)), D((nc, 16)), D((nc, 16)),
        D((nc, n_x)), D((nc, n_x)), D((nc, n_x)), D((nc, n_x)),
    ]

    def body(*refs):
        kernel(n_gx, n_gy, cap, *refs)

    def finish(*refs):
        finish_kernel(n_x, n_gy, float(8 * 8 * 32 * n_gx * n_gy) ** -0.5, *refs)

    smem = pl.BlockSpec(memory_space=pltpu.SMEM)
    vmem = pl.BlockSpec(memory_space=pltpu.VMEM)
    anywhere = pl.BlockSpec(memory_space=pl.ANY)
    parts = pl.pallas_call(
        body,
        out_shape=(
            V((slots_n, 16384), BF),
            V((16, 16, 64, 128), BF),
            V((2, n_x, tiles, 16, 128), BF),
        ),
        in_specs=[smem, smem, vmem, anywhere, anywhere, anywhere],
        out_specs=[vmem] * 3,
        scratch_shapes=scratch,
        compiler_params=pltpu.CompilerParams(
            collective_id=0, has_side_effects=True, vmem_limit_bytes=50 * 1024 * 1024
        ),
        cost_estimate=pl.CostEstimate(
            flops=12_000_000_000, bytes_accessed=20_000_000, transcendentals=0
        ),
    )(slots, inv, occupancy, features, weight.reshape(TAPS * 128, 256), cotangent)
    parts = [pltpu.with_memory_space_constraint(part, pltpu.VMEM) for part in parts]
    owned, gin, gw = pl.pallas_call(
        finish,
        out_shape=(
            jax.ShapeDtypeStruct((slots_n, 16384), BF),
            jax.ShapeDtypeStruct(features.shape, BF),
            jax.ShapeDtypeStruct(weight.shape, F32),
        ),
        in_specs=[vmem] * 3,
        out_specs=[anywhere] * 3,
        scratch_shapes=[V(weight.shape, F32), D((5,)), D((TAPS,))],
        compiler_params=pltpu.CompilerParams(vmem_limit_bytes=10 * 1024 * 1024),
        cost_estimate=pl.CostEstimate(flops=500_000_000, bytes_accessed=10_000_000, transcendentals=0),
    )(*parts)
    return owned.reshape(cotangent.shape), gin, gw


def solution(mesh):
    n_gx, n_gy = mesh.shape["gx"], mesh.shape["gy"]

    def local(*args):
        return on_device(n_gx, n_gy, *args)

    in_specs = (
        P("gx", "gy", None, None),
        P("gx", "gy", None),
        P(),
        P("gx", "gy", None),
        P("gx", "gy", None, None),
    )
    out_specs = (P("gx", "gy", None, None), P("gx", "gy", None, None), P())
    return jax.shard_map(
        local, mesh=mesh, in_specs=in_specs, out_specs=out_specs, check_vma=False
    )
```

```python
import jax
import jax.numpy as jnp
from jax import lax
from jax.experimental import pallas as pl
from jax.experimental.pallas import tpu as pltpu
from jax.sharding import PartitionSpec as P

BF = jnp.bfloat16
F32 = jnp.float32
MESH = pl.DeviceIdType.MESH
TAPS = 27
CHUNKS = ((0, 8), (8, 16), (16, 27))
SCHEDULE = (
    ("send", 0), ("weight", 0), ("weight", 1), ("sum1", 0), ("weight", 2), ("sum1", 1),
    ("sum1", 2), ("sum2", 0), ("up", 0), ("sum2", 1), ("sum3", 0), ("grad", 0),
    ("sum2", 2), ("sum3", 1), ("grad", 1), ("back1", 0), ("sum3", 2), ("send", 1),
    ("send", 2), ("back1", 1), ("grad", 2), ("back2", 0), ("back1", 2), ("grad", 3),
    ("grad", 4), ("grad", 5), ("back2", 1), ("grad", 6), ("grad", 7), ("owned", 0),
    ("back2", 2),
)
FAR_FIRST = (10, 6, 9, 11, 14, 5, 7, 13, 15, 2, 8, 1, 3, 4, 12)


def iota2(shape, dim):
    return lax.broadcasted_iota(jnp.int32, shape, dim)


def as_bf(cond):
    return jnp.where(cond, 1.0, 0.0).astype(F32).astype(BF)


def dot(a, b):
    return jnp.dot(a, b, preferred_element_type=F32)


def dot_nt(a, b):
    return lax.dot_general(a, b, (((1,), (1,)), ((), ())), preferred_element_type=F32)


def chunk_plan(n_x, n_gy):
    halves = 128 // n_x // 16
    plan, first, mine = [], 0, 0
    for t0, t1 in CHUNKS:
        used = halves * (t1 - t0)
        per = -(-used // n_gy)
        plan.append((used, per, first, mine))
        first += per * n_gy
        mine += per
    return plan, first, mine


def tile_of(plan, half, tap):
    for (t0, t1), (_, _, first, _) in zip(CHUNKS, plan):
        if t0 <= tap < t1:
            return first + half * (t1 - t0) + tap - t0


def partner(j, d):
    total, bit = 0, 1
    while bit <= 8:
        b = (j // bit) % 2
        total = total + bit * (1 - b if d & bit else b)
        bit *= 2
    return total


def row_coords(rows):
    return rows // 128, (rows // 16) % 8, (rows // 4) % 4, rows % 4


def kernel(
    n_gx, n_gy, cap,
    owner_ref, occ_ref, feat, weight, cot,
    ov, gi, ag,
    fp, pt, mk, act, bk, cv, csend, ret, outg, arr, wv, ub, yhu, ysu, uu, upt,
    xs, ys, dwf, s1s, s1r, s2s, s2r, s3s, s3r, pk, pc, po, qs, pysel,
    slot_ref, inv_ref, sem_feat, sem_in, sem_loc,
    a1_s, a1_r, a2_s, a2_r, h_s, h_r, u_s, u_r,
    r1_s, r1_r, r2_s, r2_r, r3_s, r3_r, g4_s, g4_r, g5_s, g5_r, g6_s, g6_r,
):
    n_x = n_gx // 2
    i = lax.axis_index("gx")
    j = lax.axis_index("gy")
    xq = i // 2
    core = lax.rem(i, 2)
    sib = 2 * xq + 1 - core
    nxt_i, prv_i = lax.rem(i + 1, n_gx), lax.rem(i + n_gx - 1, n_gx)
    nxt_j, prv_j = lax.rem(j + 1, n_gy), lax.rem(j + n_gy - 1, n_gy)

    cot_copy = pltpu.make_async_copy(cot.at[0, 0], cv, sem_in.at[0])
    cot_copy.start()

    def feat_copy(x):
        return pltpu.make_async_copy(feat.at[x], fp.at[x + 1, pl.ds(1, 16)], sem_feat.at[x])

    for x in range(15, -1, -1):
        feat_copy(x).start()
    w_copy = pltpu.make_async_copy(weight, wv, sem_in.at[1])
    w_copy.start()

    barrier = pltpu.get_barrier_semaphore()
    order = [d for d in FAR_FIRST if d < n_gy]
    peer_j = {d: partner(j, d) for d in order}
    peers = [(i, peer_j[d]) for d in order]
    peers += [(lax.rem(i + d, n_gx), j) for d in range(2, n_gx - 1, 2)]
    peers += [(nxt_i, j), (prv_i, j), (nxt_i, nxt_j), (prv_i, prv_j)]
    for peer in peers:
        pl.semaphore_signal(barrier, inc=1, device_id=peer, device_id_type=MESH)

    r, c = iota2((128, 256), 0), iota2((128, 256), 1)
    _, bz, vy, vz = row_coords(r)
    oz = 4 * bz + vz
    for kz in range(3):
        pk[kz] = as_bf((vy == c // 64) & (2 * oz + kz - 1 == c % 64))
    pk[3] = as_bf((vy == c // 64) & (oz == (c % 64) // 2))
    r, c = iota2((256, 256), 0), iota2((256, 256), 1)
    pc[0] = as_bf((r // 16 == c % 16) & (r % 16 == c // 16))
    pc[1] = as_bf(r == c)
    _, cbz, cvy, cvz = row_coords(c % 128)
    po[...] = as_bf((cvy == r // 64) & (8 * cbz + 2 * cvz + c // 128 == r % 64))
    rby, rbz, rvy, rvz = row_coords(r)
    cby, cbz, cvy, cvz = row_coords(c)
    roz, coz = 4 * rbz + rvz, 4 * cbz + cvz
    roy, coy = 4 * rby + rvy, 4 * cby + cvy
    qs[0] = as_bf((roy == coy) & (roz + 1 == coz))
    qs[1] = as_bf((roy + 1 == coy) & (roz == coz))
    qs[2] = as_bf((roy + 1 == coy) & (roz + 1 == coz))
    r, c = iota2((256, 128), 0), iota2((256, 128), 1)
    rby, rbz, rvy, rvz = row_coords(r)
    top = (4 * rby + rvy == 7) & (c < 32)
    qs[3, :, 0:128] = as_bf(top & (4 * rbz + rvz == c))
    qs[3, :, 128:256] = as_bf(top & (4 * rbz + rvz + 1 == c))
    r, c = iota2((128, 128), 0), iota2((128, 128), 1)
    _, cbz, cvy, cvz = row_coords(c)
    pysel[...] = as_bf((r < 32) & (cvy == 0) & (4 * cbz + cvz == r))

    def remote(src, dst, s_sem, r_sem, to):
        return pltpu.make_async_remote_copy(
            src_ref=src, dst_ref=dst, send_sem=s_sem, recv_sem=r_sem,
            device_id=to, device_id_type=MESH,
        )

    def a2a(d, src, dst, s_sem, r_sem):
        to = peer_j[d]
        return remote(
            src.at[pl.ds(to * cap, cap)], dst.at[pl.ds(j * cap, cap)], s_sem.at[d], r_sem.at[d], (i, to)
        )

    def a2a_arrival(d, src, dst, s_sem, r_sem):
        frm = peer_j[d]
        here = pl.ds(frm * cap, cap)
        return remote(src.at[here], dst.at[here], s_sem.at[d], r_sem.at[d], (i, frm))

    def occ_row(x, y):
        return occ_ref[x, pl.ds(y, 1), :].astype(F32)

    def lanes_of(rows):
        return jnp.concatenate(rows, 1)

    def wide(row):
        return jnp.broadcast_to(row, (16, 256)).astype(BF)

    def masked_rows(mat, row):
        rows = mat.shape[0]
        m = wide(row)
        return (mat.reshape(rows // 16, 16, 256) * m[None]).reshape(rows, 256)

    feat_copy(15).wait()
    for by in range(2):
        for py in range(2):
            row = lanes_of([occ_row(15, 8 * by + 2 * v + py) for v in range(4)])
            rhs = jnp.concatenate([fp[16, 1 + 8 * by + 2 * v + py] for v in range(4)], 0)
            res = dot(masked_rows(pc[1], row), rhs).astype(BF)
            for v in range(4):
                xs[8 * by + 2 * v + py] = res[64 * v : 64 * v + 64]

    for x in range(14, -1, -1):
        feat_copy(x).wait()

    def mask_y(x, carry):
        row = lanes_of([occ_row(x, 9 + 2 * v) for v in range(4)])
        rhs = jnp.concatenate([fp[x + 1, 10 + 2 * v] for v in range(4)], 0)
        ys[x] = dot(masked_rows(pc[1, 192:256, :], row), rhs).astype(BF)
        return carry

    lax.fori_loop(0, 16, mask_y, 0, unroll=4)
    pl.semaphore_wait(barrier, len(peers))
    halo_x = remote(xs, fp.at[0, pl.ds(1, 16)], h_s.at[0], h_r.at[0], (nxt_i, j))
    halo_y = remote(ys, fp.at[pl.ds(1, 16), 0], h_s.at[1], h_r.at[1], (i, nxt_j))
    halo_c = remote(ys.at[15], fp.at[0, 0], h_s.at[2], h_r.at[2], (nxt_i, nxt_j))
    halo_y.start()
    halo_x.start()
    halo_c.start()
    cot_copy.wait()

    def cot_step(n, carry):
        t, vg = n // 4, n % 4
        rhs = jnp.concatenate(
            [
                cv[pl.ds(pl.multiple_of(16 * t, 16), 16), pl.ds(pl.multiple_of(4096 * vg + 256 * v, 256), 256)]
                for v in range(16)
            ],
            0,
        )
        res = dot(pc[0], rhs).astype(BF).reshape(16, 16, 256)
        csend[pl.ds(16 * t, 16), pl.ds(pl.multiple_of(16 * vg, 16), 16), :] = res
        return carry

    lax.fori_loop(0, 12, cot_step, 0)

    for d in order:
        a2a(d, csend, ret, a1_s, a1_r).start()
    own1 = pltpu.make_async_copy(
        csend.at[pl.ds(j * cap, cap)], ret.at[pl.ds(j * cap, cap)], sem_loc.at[0]
    )
    own1.start()

    ones = jnp.ones((256, 128), F32).astype(BF)

    def prep(xp, by, ky, row, own):
        rhs = jnp.concatenate([fp[xp, 8 * by + 2 * v + ky] for v in range(4)], 0)
        with_mask = own and ky > 0
        if with_mask:
            rhs = jnp.concatenate([rhs, ones], 1)
        for kz in range(3):
            res = dot(masked_rows(pk[kz], row), rhs if kz > 0 or not with_mask else rhs[:, :128])
            col = (3 * ky + kz) * 128
            pt[xp, by * 128 : by * 128 + 128, col : col + 128] = res[:, :128].astype(BF)
            if with_mask and kz > 0:
                mk[xp - 1, 2 * (ky - 1) + kz - 1, by * 128 : by * 128 + 128, :] = res[:, 128:].astype(BF)

    def prep_own(x, carry):
        for by, ky in ((0, 1), (0, 2), (1, 0), (1, 1), (1, 2)):
            row = lanes_of([occ_row(x, 8 * by + 2 * v + ky - 1) for v in range(4)])
            prep(x + 1, by, ky, row, True)
        return carry

    lax.fori_loop(0, 16, prep_own, 0)

    def count_active(ox, carry):
        for by in range(2):
            total = jnp.zeros((1, 256), F32)
            for px in range(2):
                for py in range(2):
                    total = total + lanes_of([occ_row(2 * ox + px, 8 * by + 2 * v + py) for v in range(4)])
            count = dot(masked_rows(pk[3], total), ones)
            act[ox, by * 128 : by * 128 + 128, :] = jnp.where(count > 0.5, 1.0, 0.0).astype(BF)
        return carry

    lax.fori_loop(0, 8, count_active, 0)

    ok_x = jnp.where(i > 0, 1.0, 0.0).astype(F32)
    ok_y = jnp.where(j > 0, 1.0, 0.0).astype(F32)
    halo_x.wait()
    halo_y.wait()
    halo_c.wait()

    def prep_halo_y(x, carry):
        row = lanes_of([jnp.full((1, 64), ok_y, F32)] + [occ_row(x, 2 * v + 1) for v in range(3)])
        prep(x + 1, 0, 0, row, False)
        return carry

    lax.fori_loop(0, 16, prep_halo_y, 0)
    row_x = jnp.full((1, 256), ok_x, F32)
    corner = jnp.where(iota2((1, 256), 1) < 64, ok_x * ok_y, ok_x)
    for by in range(2):
        for ky in range(3):
            prep(0, by, ky, corner if (by == 0 and ky == 0) else row_x, False)

    w_copy.wait()

    def forward(ox, carry):
        lhs = jnp.concatenate([pt[2 * ox], pt[2 * ox + 1], pt[2 * ox + 2]], 1)
        acc = dot(lhs, wv[...])
        a = act[ox]
        a = jnp.concatenate([a, a], 1).astype(F32)
        bk[pl.ds(ox * 16, 16)] = (acc * a).astype(BF).reshape(16, 16, 256)
        return carry

    lax.fori_loop(0, 8, forward, 0)

    owners = [owner_ref[b] for b in range(32)]
    for b in range(32):
        slot = owners[b] * cap
        for earlier in range(b):
            slot = slot + jnp.where(owners[earlier] == owners[b], 1, 0)
        slot_ref[b] = slot

    def invert(s, carry):
        found = jnp.int32(0)
        for b in range(32):
            found = found + jnp.where(slot_ref[b] == s, (b // 16) * 64 + b % 16 + 1, 0)
        inv_ref[s] = found - 1
        return carry

    lax.fori_loop(0, n_gy * cap, invert, 0)

    def pack(s, carry):
        base = inv_ref[s]
        keep = jnp.where(base >= 0, 1.0, 0.0).astype(F32)
        at = jnp.maximum(base, 0)
        flag = jnp.full((16, 256), keep, F32).astype(BF)
        for vx in range(4):
            outg[s, vx * 16 : vx * 16 + 16, :] = bk[at + 16 * vx] * flag
        return carry

    lax.fori_loop(0, n_gy * cap, pack, 0)

    own1.wait()
    for d in order:
        a2a_arrival(d, csend, ret, a1_s, a1_r).wait_recv()

    def place(b, carry):
        s = slot_ref[b]
        bx, rest = b // 16, b % 16
        for vx in range(4):
            off = pl.multiple_of(rest * 16, 16)
            a = act[bx * 4 + vx, pl.ds(off, 16), :]
            a = jnp.concatenate([a, a], 1)
            ub[bx * 4 + vx, pl.ds(off, 16), :] = ret[s, vx * 16 : vx * 16 + 16, :] * a
        return carry

    lax.fori_loop(0, 32, place, 0)

    for ox in range(8):
        ysu[ox] = dot(pysel[...], ub[ox, 0:128, :])[0:32].astype(BF)
    up_x = remote(ub.at[0], ub.at[8], u_s.at[0], u_r.at[0], (prv_i, j))
    up_y = remote(ysu, yhu.at[pl.ds(0, 8)], u_s.at[1], u_r.at[1], (i, prv_j))
    up_c = remote(ysu.at[0], yhu.at[8], u_s.at[2], u_r.at[2], (prv_i, prv_j))
    up_x.start()
    up_y.start()
    up_c.start()

    own2 = pltpu.make_async_copy(
        outg.at[pl.ds(j * cap, cap)], arr.at[pl.ds(j * cap, cap)], sem_loc.at[1]
    )
    own2.start()

    def send(n):
        for d in order[5 * n : 5 * n + 5]:
            a2a(d, outg, arr, a2_s, a2_r).start()

    for ox in range(8):
        upt[:, ox * 256 : ox * 256 + 256] = dot_nt(pc[1], ub[ox]).astype(BF)

    mine = pl.multiple_of(core * 128, 128)
    other = pl.multiple_of(128 - core * 128, 128)

    rows2 = 128 // n_x
    plan, _, _ = chunk_plan(n_x, n_gy)

    def columns(n):
        return slice(CHUNKS[n][0] * 128, CHUNKS[n][1] * 128)

    def tap_rows(tap):
        kx, col = tap // 9, (tap % 9) * 128
        return jnp.concatenate([pt[2 * ox + kx, :, col : col + 128] for ox in range(8)], 0)

    def stage1(n):
        cols = columns(n)
        return remote(s1s.at[:, cols], s1r.at[:, cols], r1_s.at[n], r1_r.at[n], (sib, j))

    def weight_chunk(n):
        t0, t1 = CHUNKS[n]
        for tap in range(t0, t1, 2):
            rhs = tap_rows(tap)
            if tap + 1 < t1:
                rhs = jnp.concatenate([rhs, tap_rows(tap + 1)], 1)
            dwf[:, tap * 128 : tap * 128 + rhs.shape[1]] = dot(upt[...], rhs)
        cols = columns(n)
        s1s[:, cols] = dwf[pl.ds(other, 128), cols].astype(BF)
        stage1(n).start()

    def stage2(n, d):
        cols = columns(n)
        to = lax.rem(xq + d, n_x)
        return remote(s2s.at[to, :, cols], s2r.at[xq, :, cols], r2_s.at[n, d], r2_r.at[n, d], (2 * to + core, j))

    def stage2_arrival(n, d):
        cols = columns(n)
        frm = lax.rem(xq - d + n_x, n_x)
        return remote(s2s.at[frm, :, cols], s2r.at[frm, :, cols], r2_s.at[n, d], r2_r.at[n, d], (2 * frm + core, j))

    def after1(n):
        cols = columns(n)
        stage1(n).wait()
        for q in range(n_x):
            at = pl.multiple_of(mine + q * rows2, 16)
            mid = dwf[pl.ds(at, rows2), cols] + s1r[q * rows2 : (q + 1) * rows2, cols].astype(F32)
            dwf[pl.ds(at, rows2), cols] = mid
            s2s[q, :, cols] = mid.astype(BF)
        for d in range(1, n_x):
            stage2(n, d).start()

    def stage3(n, d):
        _, per, first, own = plan[n]
        to = peer_j[d]
        return remote(
            s3s.at[pl.ds(first + to * per, per)], s3r.at[j, pl.ds(own, per)],
            r3_s.at[n, d], r3_r.at[n, d], (i, to),
        )

    def stage3_arrival(n, d):
        _, per, first, own = plan[n]
        frm = peer_j[d]
        return remote(
            s3s.at[pl.ds(first + frm * per, per)], s3r.at[frm, pl.ds(own, per)],
            r3_s.at[n, d], r3_r.at[n, d], (i, frm),
        )

    def after2(n):
        used, per, first, _ = plan[n]
        t0, t1 = CHUNKS[n]
        cols = columns(n)
        for d in range(1, n_x):
            stage2_arrival(n, d).wait_recv()
        for half in range(rows2 // 16):
            at = pl.multiple_of(mine + xq * rows2 + half * 16, 16)
            total = dwf[pl.ds(at, 16), cols]
            for d in range(1, n_x):
                frm = lax.rem(xq + d, n_x)
                total = total + s2r[frm, half * 16 : half * 16 + 16, cols].astype(F32)
            total = total.astype(BF)
            for t in range(t1 - t0):
                s3s[first + half * (t1 - t0) + t] = total[:, t * 128 : t * 128 + 128]
        for t in range(first + used, first + per * n_gy):
            s3s[t] = jnp.zeros((16, 128), BF)
        for d in order:
            stage3(n, d).start()

    def stage4(n, d):
        _, per, first, _ = plan[n]
        here = ag.at[core, xq, pl.ds(first + j * per, per)]
        return remote(here, here, g4_s.at[n, d], g4_r.at[n, d], (i, peer_j[d]))

    def stage4_arrival(n, d):
        _, per, first, _ = plan[n]
        here = ag.at[core, xq, pl.ds(first + peer_j[d] * per, per)]
        return remote(here, here, g4_s.at[n, d], g4_r.at[n, d], (i, peer_j[d]))

    def after3(n):
        _, per, first, own = plan[n]
        for d in order:
            stage3_arrival(n, d).wait_recv()
        total = s3s[pl.ds(first + j * per, per)].astype(F32)
        for d in order:
            total = total + s3r[peer_j[d], own : own + per].astype(F32)
        ag[core, xq, pl.ds(first + j * per, per)] = total.astype(BF)
        for d in order:
            stage4(n, d).start()

    def block(c, q, n):
        used, _, first, _ = plan[n]
        return ag.at[c, q, first : first + used]

    def stage5(n, d):
        to = lax.rem(xq + d, n_x)
        here = block(core, xq, n)
        return remote(here, here, g5_s.at[n, d], g5_r.at[n, d], (2 * to + core, j))

    def stage5_arrival(n, d):
        frm = lax.rem(xq - d + n_x, n_x)
        here = block(core, frm, n)
        return remote(here, here, g5_s.at[n, d], g5_r.at[n, d], (2 * frm + core, j))

    def stage6(n, d):
        here = block(core, lax.rem(xq - d + n_x, n_x), n)
        return remote(here, here, g6_s.at[n, d], g6_r.at[n, d], (sib, j))

    def stage6_arrival(n, d):
        here = block(1 - core, lax.rem(xq - d + n_x, n_x), n)
        return remote(here, here, g6_s.at[n, d], g6_r.at[n, d], (sib, j))

    def after4(n):
        for d in order:
            stage4_arrival(n, d).wait_recv()
        for d in range(1, n_x):
            stage5(n, d).start()
        stage6(n, 0).start()

    def after5(n):
        for d in range(1, n_x):
            stage5_arrival(n, d).wait_recv()
            stage6(n, d).start()

    okn_x = jnp.where(i < n_gx - 1, 1.0, 0.0).astype(F32)
    okn_y = jnp.where(j < n_gy - 1, 1.0, 0.0).astype(F32)

    def shifts(ox, carry):
        last = jnp.where(ox == 8, okn_x, 1.0).astype(F32)
        base = (ub[ox].astype(F32) * last).astype(BF)
        halo = (yhu[ox].astype(F32) * (last * okn_y)).astype(BF)
        halo = jnp.concatenate([halo, jnp.zeros((96, 256), BF)], 0)
        uu[0, ox, :, 0:256] = base
        uu[0, ox, :, 256:512] = dot(qs[0], base).astype(BF)
        uu[1, ox, :, 0:256] = (dot(qs[1], base) + dot(qs[3, :, 0:128], halo)).astype(BF)
        uu[1, ox, :, 256:512] = (dot(qs[2], base) + dot(qs[3, :, 128:256], halo)).astype(BF)
        return carry

    def shift_all(n):
        up_x.wait()
        up_y.wait()
        up_c.wait()
        lax.fori_loop(0, 9, shifts, 0, unroll=3)

    lists = (((1, 0),), ((2, 0), (0, 1)))

    def grad_in(ox, carry):
        for px in range(2):
            for py in range(2):
                both, odd = None, None
                for a, sx in lists[px]:
                    for b, sy in lists[py]:
                        k = 9 * a + 3 * b
                        one = dot_nt(uu[sy, ox + sx, :, 0:256], wv[(k + 1) * 128 : (k + 3) * 128, :])
                        two = dot_nt(uu[sy, ox + sx, :, 256:512], wv[k * 128 : (k + 1) * 128, :])
                        both = one if both is None else both + one
                        odd = two if odd is None else odd + two
                m0 = mk[2 * ox + px, 2 * py].astype(F32)
                m1 = mk[2 * ox + px, 2 * py + 1].astype(F32)
                g0 = (both[:, :128] * m0).astype(BF)
                g1 = ((both[:, 128:] + odd) * m1).astype(BF)
                rhs = jnp.concatenate(
                    [
                        jnp.concatenate([g0[:128], g1[:128]], 0),
                        jnp.concatenate([g0[128:], g1[128:]], 0),
                    ],
                    1,
                )
                res = dot(po[...], rhs).astype(BF)
                for by in range(2):
                    for v in range(4):
                        gi[2 * ox + px, 8 * by + 2 * v + py] = res[64 * v : 64 * v + 64, 128 * by : 128 * by + 128]
        return carry

    def one_grad(n):
        grad_in(n, 0)

    def owned_step(n, carry):
        t, vg = n // 4, n % 4
        rhs = arr[pl.ds(16 * t, 16), pl.ds(pl.multiple_of(16 * vg, 16), 16), :].reshape(256, 256)
        res = dot(pc[0], rhs).astype(BF)
        for v in range(16):
            ov[pl.ds(pl.multiple_of(16 * t, 16), 16), pl.ds(pl.multiple_of(4096 * vg + 256 * v, 256), 256)] = res[16 * v : 16 * v + 16]
        return carry

    def owned(n):
        own2.wait()
        for d in order:
            a2a_arrival(d, outg, arr, a2_s, a2_r).wait_recv()
        lax.fori_loop(0, 12, owned_step, 0, unroll=2)

    steps = dict(
        weight=weight_chunk, sum1=after1, sum2=after2, sum3=after3, back1=after4, back2=after5,
        up=shift_all, grad=one_grad, send=send, owned=owned,
    )
    for step, n in SCHEDULE:
        steps[step](n)
    for n in range(len(CHUNKS)):
        for d in range(n_x):
            stage6_arrival(n, d).wait_recv()

    for d in order:
        a2a(d, csend, ret, a1_s, a1_r).wait_send()
        a2a(d, outg, arr, a2_s, a2_r).wait_send()
    for n in range(len(CHUNKS)):
        for d in order:
            stage3(n, d).wait_send()
            stage4(n, d).wait_send()
        for d in range(1, n_x):
            stage2(n, d).wait_send()
            stage5(n, d).wait_send()
        for d in range(n_x):
            stage6(n, d).wait_send()


def finish_kernel(n_x, n_gy, scale, ov, gi, ag, owned_out, gin_out, gw_out, gws, sem_big, sem_gw):
    plan, _, _ = chunk_plan(n_x, n_gy)
    copies = [pltpu.make_async_copy(gi.at[pl.ds(4 * n, 4)], gin_out.at[pl.ds(4 * n, 4)], sem_big.at[n]) for n in range(4)]
    copies.append(pltpu.make_async_copy(ov, owned_out, sem_big.at[4]))
    for copy in copies:
        copy.start()
    eye = as_bf(iota2((128, 128), 0) == iota2((128, 128), 1))
    for tap in range(TAPS):
        rows = jnp.concatenate(
            [
                ag[c, q, tile_of(plan, half, tap)]
                for c in range(2)
                for q in range(n_x)
                for half in range(128 // n_x // 16)
            ],
            0,
        )
        gws[tap] = dot_nt(eye, rows) * scale
        copy = pltpu.make_async_copy(gws.at[tap], gw_out.at[tap], sem_gw.at[tap])
        copy.start()
        copies.append(copy)
    for copy in copies:
        copy.wait()


def on_device(n_gx, n_gy, features, occupancy, weight, owner, cotangent):
    cap = cotangent.shape[2] // n_gy
    n_x = n_gx // 2
    rows2 = 128 // n_x
    _, tiles, per = chunk_plan(n_x, n_gy)
    slots_n = n_gy * cap

    V = pltpu.VMEM
    D = pltpu.SemaphoreType.DMA
    nc = len(CHUNKS)
    scratch = [
        V((17, 17, 64, 128), BF),
        V((17, 256, 1152), BF),
        V((16, 4, 256, 128), BF),
        V((8, 256, 128), BF),
        V((128, 16, 256), BF),
        V((slots_n, 16384), BF),
        V((slots_n, 64, 256), BF),
        V((slots_n, 64, 256), BF),
        V((slots_n, 64, 256), BF),
        V((slots_n, 64, 256), BF),
        V((TAPS * 128, 256), BF),
        V((9, 256, 256), BF),
        V((9, 32, 256), BF),
        V((8, 32, 256), BF),
        V((2, 9, 256, 512), BF),
        V((256, 2048), BF),
        V((16, 64, 128), BF),
        V((16, 64, 128), BF),
        V((256, TAPS * 128), F32),
        V((128, TAPS * 128), BF),
        V((128, TAPS * 128), BF),
        V((n_x, rows2, TAPS * 128), BF),
        V((n_x, rows2, TAPS * 128), BF),
        V((tiles, 16, 128), BF),
        V((n_gy, per, 16, 128), BF),
        V((4, 128, 256), BF),
        V((2, 256, 256), BF),
        V((256, 256), BF),
        V((4, 256, 256), BF),
        V((128, 128), BF),
        pltpu.SMEM((32,), jnp.int32),
        pltpu.SMEM((slots_n,), jnp.int32),
        D((16,)), D((2,)), D((2,)),
        D((16,)), D((16,)), D((16,)), D((16,)),
        D((3,)), D((3,)), D((3,)), D((3,)),
        D((nc,)), D((nc,)), D((nc, n_x)), D((nc, n_x)),
        D((nc, 16)), D((nc, 16)), D((nc, 16)), D((nc, 16)),
        D((nc, n_x)), D((nc, n_x)), D((nc, n_x)), D((nc, n_x)),
    ]

    def body(*refs):
        kernel(n_gx, n_gy, cap, *refs)

    def finish(*refs):
        finish_kernel(n_x, n_gy, float(8 * 8 * 32 * n_gx * n_gy) ** -0.5, *refs)

    smem = pl.BlockSpec(memory_space=pltpu.SMEM)
    vmem = pl.BlockSpec(memory_space=pltpu.VMEM)
    anywhere = pl.BlockSpec(memory_space=pl.ANY)
    parts = pl.pallas_call(
        body,
        out_shape=(
            V((slots_n, 16384), BF),
            V((16, 16, 64, 128), BF),
            V((2, n_x, tiles, 16, 128), BF),
        ),
        in_specs=[smem, vmem, anywhere, anywhere, anywhere],
        out_specs=[vmem] * 3,
        scratch_shapes=scratch,
        compiler_params=pltpu.CompilerParams(
            collective_id=0, has_side_effects=True, vmem_limit_bytes=50 * 1024 * 1024
        ),
        cost_estimate=pl.CostEstimate(
            flops=12_000_000_000, bytes_accessed=20_000_000, transcendentals=0
        ),
    )(owner.reshape(32), occupancy, features, weight.reshape(TAPS * 128, 256), cotangent)
    parts = [pltpu.with_memory_space_constraint(part, pltpu.VMEM) for part in parts]
    owned, gin, gw = pl.pallas_call(
        finish,
        out_shape=(
            jax.ShapeDtypeStruct((slots_n, 16384), BF),
            jax.ShapeDtypeStruct(features.shape, BF),
            jax.ShapeDtypeStruct(weight.shape, F32),
        ),
        in_specs=[vmem] * 3,
        out_specs=[anywhere] * 3,
        scratch_shapes=[V(weight.shape, F32), D((5,)), D((TAPS,))],
        compiler_params=pltpu.CompilerParams(vmem_limit_bytes=10 * 1024 * 1024),
        cost_estimate=pl.CostEstimate(flops=500_000_000, bytes_accessed=10_000_000, transcendentals=0),
    )(*parts)
    return owned.reshape(cotangent.shape), gin, gw


def solution(mesh):
    n_gx, n_gy = mesh.shape["gx"], mesh.shape["gy"]

    def local(*args):
        return on_device(n_gx, n_gy, *args)

    in_specs = (
        P("gx", "gy", None, None),
        P("gx", "gy", None),
        P(),
        P("gx", "gy", None),
        P("gx", "gy", None, None),
    )
    out_specs = (P("gx", "gy", None, None), P("gx", "gy", None, None), P())
    return jax.shard_map(
        local, mesh=mesh, in_specs=in_specs, out_specs=out_specs, check_vma=False
    )
```

```python
import jax
import jax.numpy as jnp
from jax import lax
from jax.experimental import pallas as pl
from jax.experimental.pallas import tpu as pltpu
from jax.sharding import PartitionSpec as P

BF = jnp.bfloat16
F32 = jnp.float32
MESH = pl.DeviceIdType.MESH
TAPS = 27
CHUNKS = ((0, 8), (8, 16), (16, 27))
SCHEDULE = (
    ("send", 0), ("weight", 0), ("weight", 1), ("sum1", 0), ("weight", 2), ("sum1", 1),
    ("sum1", 2), ("sum2", 0), ("up", 0), ("sum2", 1), ("sum3", 0), ("grad", 0),
    ("sum2", 2), ("sum3", 1), ("grad", 1), ("back1", 0), ("sum3", 2), ("send", 1),
    ("send", 2), ("back1", 1), ("grad", 2), ("back2", 0), ("back1", 2), ("grad", 3),
    ("grad", 4), ("grad", 5), ("back2", 1), ("grad", 6), ("grad", 7), ("back2", 2),
    ("owned", 0),
)
FAR_FIRST = (10, 6, 9, 11, 14, 5, 7, 13, 15, 2, 8, 1, 3, 4, 12)


def iota2(shape, dim):
    return lax.broadcasted_iota(jnp.int32, shape, dim)


def as_bf(cond):
    return jnp.where(cond, 1.0, 0.0).astype(F32).astype(BF)


def dot(a, b):
    return jnp.dot(a, b, preferred_element_type=F32)


def dot_nt(a, b):
    return lax.dot_general(a, b, (((1,), (1,)), ((), ())), preferred_element_type=F32)


def chunk_plan(n_x, n_gy):
    halves = 128 // n_x // 16
    plan, first, mine = [], 0, 0
    for t0, t1 in CHUNKS:
        used = halves * (t1 - t0)
        per = -(-used // n_gy)
        plan.append((used, per, first, mine))
        first += per * n_gy
        mine += per
    return plan, first, mine


def tile_of(plan, half, tap):
    for (t0, t1), (_, _, first, _) in zip(CHUNKS, plan):
        if t0 <= tap < t1:
            return first + half * (t1 - t0) + tap - t0


def partner(j, d):
    total, bit = 0, 1
    while bit <= 8:
        b = (j // bit) % 2
        total = total + bit * (1 - b if d & bit else b)
        bit *= 2
    return total


def row_coords(rows):
    return rows // 128, (rows // 16) % 8, (rows // 4) % 4, rows % 4


def kernel(
    n_gx, n_gy, cap,
    owner_ref, occ_ref, feat, weight, cot,
    ov, gi, ag,
    fp, pt, mk, act, bk, cv, csend, ret, outg, arr, wv, ub, yhu, ysu, uu, upt,
    xs, ys, dwf, s1s, s1r, s2s, s2r, s3s, s3r, pk, pc, po, qs, pysel,
    slot_ref, inv_ref, sem_feat, sem_in, sem_loc,
    a1_s, a1_r, a2_s, a2_r, h_s, h_r, u_s, u_r,
    r1_s, r1_r, r2_s, r2_r, r3_s, r3_r, g4_s, g4_r, g5_s, g5_r, g6_s, g6_r,
):
    n_x = n_gx // 2
    i = lax.axis_index("gx")
    j = lax.axis_index("gy")
    xq = i // 2
    core = lax.rem(i, 2)
    sib = 2 * xq + 1 - core
    nxt_i, prv_i = lax.rem(i + 1, n_gx), lax.rem(i + n_gx - 1, n_gx)
    nxt_j, prv_j = lax.rem(j + 1, n_gy), lax.rem(j + n_gy - 1, n_gy)

    cot_copy = pltpu.make_async_copy(cot.at[0, 0], cv, sem_in.at[0])
    cot_copy.start()

    def feat_copy(x):
        return pltpu.make_async_copy(feat.at[x], fp.at[x + 1, pl.ds(1, 16)], sem_feat.at[x])

    for x in range(15, -1, -1):
        feat_copy(x).start()
    w_copy = pltpu.make_async_copy(weight, wv, sem_in.at[1])
    w_copy.start()

    barrier = pltpu.get_barrier_semaphore()
    order = [d for d in FAR_FIRST if d < n_gy]
    peer_j = {d: partner(j, d) for d in order}
    peers = [(i, peer_j[d]) for d in order]
    peers += [(lax.rem(i + d, n_gx), j) for d in range(2, n_gx - 1, 2)]
    peers += [(nxt_i, j), (prv_i, j), (nxt_i, nxt_j), (prv_i, prv_j)]
    for peer in peers:
        pl.semaphore_signal(barrier, inc=1, device_id=peer, device_id_type=MESH)

    r, c = iota2((128, 256), 0), iota2((128, 256), 1)
    _, bz, vy, vz = row_coords(r)
    oz = 4 * bz + vz
    for kz in range(3):
        pk[kz] = as_bf((vy == c // 64) & (2 * oz + kz - 1 == c % 64))
    pk[3] = as_bf((vy == c // 64) & (oz == (c % 64) // 2))
    r, c = iota2((256, 256), 0), iota2((256, 256), 1)
    pc[0] = as_bf((r // 16 == c % 16) & (r % 16 == c // 16))
    pc[1] = as_bf(r == c)
    _, cbz, cvy, cvz = row_coords(c % 128)
    po[...] = as_bf((cvy == r // 64) & (8 * cbz + 2 * cvz + c // 128 == r % 64))
    rby, rbz, rvy, rvz = row_coords(r)
    cby, cbz, cvy, cvz = row_coords(c)
    roz, coz = 4 * rbz + rvz, 4 * cbz + cvz
    roy, coy = 4 * rby + rvy, 4 * cby + cvy
    qs[0] = as_bf((roy == coy) & (roz + 1 == coz))
    qs[1] = as_bf((roy + 1 == coy) & (roz == coz))
    qs[2] = as_bf((roy + 1 == coy) & (roz + 1 == coz))
    r, c = iota2((256, 128), 0), iota2((256, 128), 1)
    rby, rbz, rvy, rvz = row_coords(r)
    top = (4 * rby + rvy == 7) & (c < 32)
    qs[3, :, 0:128] = as_bf(top & (4 * rbz + rvz == c))
    qs[3, :, 128:256] = as_bf(top & (4 * rbz + rvz + 1 == c))
    r, c = iota2((128, 128), 0), iota2((128, 128), 1)
    _, cbz, cvy, cvz = row_coords(c)
    pysel[...] = as_bf((r < 32) & (cvy == 0) & (4 * cbz + cvz == r))

    def remote(src, dst, s_sem, r_sem, to):
        return pltpu.make_async_remote_copy(
            src_ref=src, dst_ref=dst, send_sem=s_sem, recv_sem=r_sem,
            device_id=to, device_id_type=MESH,
        )

    def a2a(d, src, dst, s_sem, r_sem):
        to = peer_j[d]
        return remote(
            src.at[pl.ds(to * cap, cap)], dst.at[pl.ds(j * cap, cap)], s_sem.at[d], r_sem.at[d], (i, to)
        )

    def a2a_arrival(d, src, dst, s_sem, r_sem):
        frm = peer_j[d]
        here = pl.ds(frm * cap, cap)
        return remote(src.at[here], dst.at[here], s_sem.at[d], r_sem.at[d], (i, frm))

    def occ_row(x, y):
        return occ_ref[x, pl.ds(y, 1), :].astype(F32)

    def lanes_of(rows):
        return jnp.concatenate(rows, 1)

    def wide(row):
        return jnp.broadcast_to(row, (16, 256)).astype(BF)

    def masked_rows(mat, row):
        rows = mat.shape[0]
        m = wide(row)
        return (mat.reshape(rows // 16, 16, 256) * m[None]).reshape(rows, 256)

    feat_copy(15).wait()
    for by in range(2):
        for py in range(2):
            row = lanes_of([occ_row(15, 8 * by + 2 * v + py) for v in range(4)])
            rhs = jnp.concatenate([fp[16, 1 + 8 * by + 2 * v + py] for v in range(4)], 0)
            res = dot(masked_rows(pc[1], row), rhs).astype(BF)
            for v in range(4):
                xs[8 * by + 2 * v + py] = res[64 * v : 64 * v + 64]

    for x in range(14, -1, -1):
        feat_copy(x).wait()

    def mask_y(x, carry):
        row = lanes_of([occ_row(x, 9 + 2 * v) for v in range(4)])
        rhs = jnp.concatenate([fp[x + 1, 10 + 2 * v] for v in range(4)], 0)
        ys[x] = dot(masked_rows(pc[1, 192:256, :], row), rhs).astype(BF)
        return carry

    lax.fori_loop(0, 16, mask_y, 0, unroll=4)
    pl.semaphore_wait(barrier, len(peers))
    halo_x = remote(xs, fp.at[0, pl.ds(1, 16)], h_s.at[0], h_r.at[0], (nxt_i, j))
    halo_y = remote(ys, fp.at[pl.ds(1, 16), 0], h_s.at[1], h_r.at[1], (i, nxt_j))
    halo_c = remote(ys.at[15], fp.at[0, 0], h_s.at[2], h_r.at[2], (nxt_i, nxt_j))
    halo_y.start()
    halo_x.start()
    halo_c.start()
    cot_copy.wait()

    def cot_step(n, carry):
        t, vg = n // 4, n % 4
        rhs = jnp.concatenate(
            [
                cv[pl.ds(pl.multiple_of(16 * t, 16), 16), pl.ds(pl.multiple_of(4096 * vg + 256 * v, 256), 256)]
                for v in range(16)
            ],
            0,
        )
        res = dot(pc[0], rhs).astype(BF).reshape(16, 16, 256)
        csend[pl.ds(16 * t, 16), pl.ds(pl.multiple_of(16 * vg, 16), 16), :] = res
        return carry

    lax.fori_loop(0, 12, cot_step, 0)

    for d in order:
        a2a(d, csend, ret, a1_s, a1_r).start()
    own1 = pltpu.make_async_copy(
        csend.at[pl.ds(j * cap, cap)], ret.at[pl.ds(j * cap, cap)], sem_loc.at[0]
    )
    own1.start()

    ones = jnp.ones((256, 128), F32).astype(BF)

    def prep(xp, by, ky, row, own):
        rhs = jnp.concatenate([fp[xp, 8 * by + 2 * v + ky] for v in range(4)], 0)
        with_mask = own and ky > 0
        if with_mask:
            rhs = jnp.concatenate([rhs, ones], 1)
        for kz in range(3):
            res = dot(masked_rows(pk[kz], row), rhs if kz > 0 or not with_mask else rhs[:, :128])
            col = (3 * ky + kz) * 128
            pt[xp, by * 128 : by * 128 + 128, col : col + 128] = res[:, :128].astype(BF)
            if with_mask and kz > 0:
                mk[xp - 1, 2 * (ky - 1) + kz - 1, by * 128 : by * 128 + 128, :] = res[:, 128:].astype(BF)

    def prep_own(x, carry):
        for by, ky in ((0, 1), (0, 2), (1, 0), (1, 1), (1, 2)):
            row = lanes_of([occ_row(x, 8 * by + 2 * v + ky - 1) for v in range(4)])
            prep(x + 1, by, ky, row, True)
        return carry

    lax.fori_loop(0, 16, prep_own, 0)

    def count_active(ox, carry):
        for by in range(2):
            total = jnp.zeros((1, 256), F32)
            for px in range(2):
                for py in range(2):
                    total = total + lanes_of([occ_row(2 * ox + px, 8 * by + 2 * v + py) for v in range(4)])
            count = dot(masked_rows(pk[3], total), ones)
            act[ox, by * 128 : by * 128 + 128, :] = jnp.where(count > 0.5, 1.0, 0.0).astype(BF)
        return carry

    lax.fori_loop(0, 8, count_active, 0)

    ok_x = jnp.where(i > 0, 1.0, 0.0).astype(F32)
    ok_y = jnp.where(j > 0, 1.0, 0.0).astype(F32)
    halo_x.wait()
    halo_y.wait()
    halo_c.wait()

    def prep_halo_y(x, carry):
        row = lanes_of([jnp.full((1, 64), ok_y, F32)] + [occ_row(x, 2 * v + 1) for v in range(3)])
        prep(x + 1, 0, 0, row, False)
        return carry

    lax.fori_loop(0, 16, prep_halo_y, 0)
    row_x = jnp.full((1, 256), ok_x, F32)
    corner = jnp.where(iota2((1, 256), 1) < 64, ok_x * ok_y, ok_x)
    for by in range(2):
        for ky in range(3):
            prep(0, by, ky, corner if (by == 0 and ky == 0) else row_x, False)

    w_copy.wait()

    def forward(ox, carry):
        lhs = jnp.concatenate([pt[2 * ox], pt[2 * ox + 1], pt[2 * ox + 2]], 1)
        acc = dot(lhs, wv[...])
        a = act[ox]
        a = jnp.concatenate([a, a], 1).astype(F32)
        bk[pl.ds(ox * 16, 16)] = (acc * a).astype(BF).reshape(16, 16, 256)
        return carry

    lax.fori_loop(0, 8, forward, 0)

    owners = [owner_ref[b] for b in range(32)]
    for b in range(32):
        slot = owners[b] * cap
        for earlier in range(b):
            slot = slot + jnp.where(owners[earlier] == owners[b], 1, 0)
        slot_ref[b] = slot

    def invert(s, carry):
        found = jnp.int32(0)
        for b in range(32):
            found = found + jnp.where(slot_ref[b] == s, (b // 16) * 64 + b % 16 + 1, 0)
        inv_ref[s] = found - 1
        return carry

    lax.fori_loop(0, n_gy * cap, invert, 0)

    def pack(s, carry):
        base = inv_ref[s]
        keep = jnp.where(base >= 0, 1.0, 0.0).astype(F32)
        at = jnp.maximum(base, 0)
        flag = jnp.full((16, 256), keep, F32).astype(BF)
        for vx in range(4):
            outg[s, vx * 16 : vx * 16 + 16, :] = bk[at + 16 * vx] * flag
        return carry

    lax.fori_loop(0, n_gy * cap, pack, 0)

    own1.wait()
    for d in order:
        a2a_arrival(d, csend, ret, a1_s, a1_r).wait_recv()

    def place(b, carry):
        s = slot_ref[b]
        bx, rest = b // 16, b % 16
        for vx in range(4):
            off = pl.multiple_of(rest * 16, 16)
            a = act[bx * 4 + vx, pl.ds(off, 16), :]
            a = jnp.concatenate([a, a], 1)
            ub[bx * 4 + vx, pl.ds(off, 16), :] = ret[s, vx * 16 : vx * 16 + 16, :] * a
        return carry

    lax.fori_loop(0, 32, place, 0)

    for ox in range(8):
        ysu[ox] = dot(pysel[...], ub[ox, 0:128, :])[0:32].astype(BF)
    up_x = remote(ub.at[0], ub.at[8], u_s.at[0], u_r.at[0], (prv_i, j))
    up_y = remote(ysu, yhu.at[pl.ds(0, 8)], u_s.at[1], u_r.at[1], (i, prv_j))
    up_c = remote(ysu.at[0], yhu.at[8], u_s.at[2], u_r.at[2], (prv_i, prv_j))
    up_x.start()
    up_y.start()
    up_c.start()

    own2 = pltpu.make_async_copy(
        outg.at[pl.ds(j * cap, cap)], arr.at[pl.ds(j * cap, cap)], sem_loc.at[1]
    )
    own2.start()

    def send(n):
        for d in order[5 * n : 5 * n + 5]:
            a2a(d, outg, arr, a2_s, a2_r).start()

    for ox in range(8):
        upt[:, ox * 256 : ox * 256 + 256] = dot_nt(pc[1], ub[ox]).astype(BF)

    mine = pl.multiple_of(core * 128, 128)
    other = pl.multiple_of(128 - core * 128, 128)

    rows2 = 128 // n_x
    plan, _, _ = chunk_plan(n_x, n_gy)

    def columns(n):
        return slice(CHUNKS[n][0] * 128, CHUNKS[n][1] * 128)

    def tap_rows(tap):
        kx, col = tap // 9, (tap % 9) * 128
        return jnp.concatenate([pt[2 * ox + kx, :, col : col + 128] for ox in range(8)], 0)

    def stage1(n):
        cols = columns(n)
        return remote(s1s.at[:, cols], s1r.at[:, cols], r1_s.at[n], r1_r.at[n], (sib, j))

    def weight_chunk(n):
        t0, t1 = CHUNKS[n]
        for tap in range(t0, t1, 2):
            rhs = tap_rows(tap)
            if tap + 1 < t1:
                rhs = jnp.concatenate([rhs, tap_rows(tap + 1)], 1)
            dwf[:, tap * 128 : tap * 128 + rhs.shape[1]] = dot(upt[...], rhs)
        cols = columns(n)
        s1s[:, cols] = dwf[pl.ds(other, 128), cols].astype(BF)
        stage1(n).start()

    def stage2(n, d):
        cols = columns(n)
        to = lax.rem(xq + d, n_x)
        return remote(s2s.at[to, :, cols], s2r.at[xq, :, cols], r2_s.at[n, d], r2_r.at[n, d], (2 * to + core, j))

    def stage2_arrival(n, d):
        cols = columns(n)
        frm = lax.rem(xq - d + n_x, n_x)
        return remote(s2s.at[frm, :, cols], s2r.at[frm, :, cols], r2_s.at[n, d], r2_r.at[n, d], (2 * frm + core, j))

    def after1(n):
        cols = columns(n)
        stage1(n).wait()
        for q in range(n_x):
            at = pl.multiple_of(mine + q * rows2, 16)
            mid = dwf[pl.ds(at, rows2), cols] + s1r[q * rows2 : (q + 1) * rows2, cols].astype(F32)
            dwf[pl.ds(at, rows2), cols] = mid
            s2s[q, :, cols] = mid.astype(BF)
        for d in range(1, n_x):
            stage2(n, d).start()

    def stage3(n, d):
        _, per, first, own = plan[n]
        to = peer_j[d]
        return remote(
            s3s.at[pl.ds(first + to * per, per)], s3r.at[j, pl.ds(own, per)],
            r3_s.at[n, d], r3_r.at[n, d], (i, to),
        )

    def stage3_arrival(n, d):
        _, per, first, own = plan[n]
        frm = peer_j[d]
        return remote(
            s3s.at[pl.ds(first + frm * per, per)], s3r.at[frm, pl.ds(own, per)],
            r3_s.at[n, d], r3_r.at[n, d], (i, frm),
        )

    def after2(n):
        used, per, first, _ = plan[n]
        t0, t1 = CHUNKS[n]
        cols = columns(n)
        for d in range(1, n_x):
            stage2_arrival(n, d).wait_recv()
        for half in range(rows2 // 16):
            at = pl.multiple_of(mine + xq * rows2 + half * 16, 16)
            total = dwf[pl.ds(at, 16), cols]
            for d in range(1, n_x):
                frm = lax.rem(xq + d, n_x)
                total = total + s2r[frm, half * 16 : half * 16 + 16, cols].astype(F32)
            total = total.astype(BF)
            for t in range(t1 - t0):
                s3s[first + half * (t1 - t0) + t] = total[:, t * 128 : t * 128 + 128]
        for t in range(first + used, first + per * n_gy):
            s3s[t] = jnp.zeros((16, 128), BF)
        for d in order:
            stage3(n, d).start()

    def stage4(n, d):
        _, per, first, _ = plan[n]
        here = ag.at[core, xq, pl.ds(first + j * per, per)]
        return remote(here, here, g4_s.at[n, d], g4_r.at[n, d], (i, peer_j[d]))

    def stage4_arrival(n, d):
        _, per, first, _ = plan[n]
        here = ag.at[core, xq, pl.ds(first + peer_j[d] * per, per)]
        return remote(here, here, g4_s.at[n, d], g4_r.at[n, d], (i, peer_j[d]))

    def after3(n):
        _, per, first, own = plan[n]
        for d in order:
            stage3_arrival(n, d).wait_recv()
        total = s3s[pl.ds(first + j * per, per)].astype(F32)
        for d in order:
            total = total + s3r[peer_j[d], own : own + per].astype(F32)
        ag[core, xq, pl.ds(first + j * per, per)] = total.astype(BF)
        for d in order:
            stage4(n, d).start()

    def block(c, q, n):
        used, _, first, _ = plan[n]
        return ag.at[c, q, first : first + used]

    def stage5(n, d):
        to = lax.rem(xq + d, n_x)
        here = block(core, xq, n)
        return remote(here, here, g5_s.at[n, d], g5_r.at[n, d], (2 * to + core, j))

    def stage5_arrival(n, d):
        frm = lax.rem(xq - d + n_x, n_x)
        here = block(core, frm, n)
        return remote(here, here, g5_s.at[n, d], g5_r.at[n, d], (2 * frm + core, j))

    def stage6(n, d):
        here = block(core, lax.rem(xq - d + n_x, n_x), n)
        return remote(here, here, g6_s.at[n, d], g6_r.at[n, d], (sib, j))

    def stage6_arrival(n, d):
        here = block(1 - core, lax.rem(xq - d + n_x, n_x), n)
        return remote(here, here, g6_s.at[n, d], g6_r.at[n, d], (sib, j))

    def after4(n):
        for d in order:
            stage4_arrival(n, d).wait_recv()
        for d in range(1, n_x):
            stage5(n, d).start()
        stage6(n, 0).start()

    def after5(n):
        for d in range(1, n_x):
            stage5_arrival(n, d).wait_recv()
            stage6(n, d).start()

    okn_x = jnp.where(i < n_gx - 1, 1.0, 0.0).astype(F32)
    okn_y = jnp.where(j < n_gy - 1, 1.0, 0.0).astype(F32)

    def shifts(ox, carry):
        last = jnp.where(ox == 8, okn_x, 1.0).astype(F32)
        base = (ub[ox].astype(F32) * last).astype(BF)
        halo = (yhu[ox].astype(F32) * (last * okn_y)).astype(BF)
        halo = jnp.concatenate([halo, jnp.zeros((96, 256), BF)], 0)
        uu[0, ox, :, 0:256] = base
        uu[0, ox, :, 256:512] = dot(qs[0], base).astype(BF)
        uu[1, ox, :, 0:256] = (dot(qs[1], base) + dot(qs[3, :, 0:128], halo)).astype(BF)
        uu[1, ox, :, 256:512] = (dot(qs[2], base) + dot(qs[3, :, 128:256], halo)).astype(BF)
        return carry

    def shift_all(n):
        up_x.wait()
        up_y.wait()
        up_c.wait()
        lax.fori_loop(0, 9, shifts, 0, unroll=3)

    lists = (((1, 0),), ((2, 0), (0, 1)))

    def grad_in(ox, carry):
        for px in range(2):
            for py in range(2):
                both, odd = None, None
                for a, sx in lists[px]:
                    for b, sy in lists[py]:
                        k = 9 * a + 3 * b
                        one = dot_nt(uu[sy, ox + sx, :, 0:256], wv[(k + 1) * 128 : (k + 3) * 128, :])
                        two = dot_nt(uu[sy, ox + sx, :, 256:512], wv[k * 128 : (k + 1) * 128, :])
                        both = one if both is None else both + one
                        odd = two if odd is None else odd + two
                m0 = mk[2 * ox + px, 2 * py].astype(F32)
                m1 = mk[2 * ox + px, 2 * py + 1].astype(F32)
                g0 = (both[:, :128] * m0).astype(BF)
                g1 = ((both[:, 128:] + odd) * m1).astype(BF)
                rhs = jnp.concatenate(
                    [
                        jnp.concatenate([g0[:128], g1[:128]], 0),
                        jnp.concatenate([g0[128:], g1[128:]], 0),
                    ],
                    1,
                )
                res = dot(po[...], rhs).astype(BF)
                for by in range(2):
                    for v in range(4):
                        gi[2 * ox + px, 8 * by + 2 * v + py] = res[64 * v : 64 * v + 64, 128 * by : 128 * by + 128]
        return carry

    def one_grad(n):
        grad_in(n, 0)

    def owned_step(n, carry):
        t, vg = n // 4, n % 4
        rhs = arr[pl.ds(16 * t, 16), pl.ds(pl.multiple_of(16 * vg, 16), 16), :].reshape(256, 256)
        res = dot(pc[0], rhs).astype(BF)
        for v in range(16):
            ov[pl.ds(pl.multiple_of(16 * t, 16), 16), pl.ds(pl.multiple_of(4096 * vg + 256 * v, 256), 256)] = res[16 * v : 16 * v + 16]
        return carry

    def owned(n):
        own2.wait()
        for d in order:
            a2a_arrival(d, outg, arr, a2_s, a2_r).wait_recv()
        lax.fori_loop(0, 12, owned_step, 0, unroll=2)

    steps = dict(
        weight=weight_chunk, sum1=after1, sum2=after2, sum3=after3, back1=after4, back2=after5,
        up=shift_all, grad=one_grad, send=send, owned=owned,
    )
    for step, n in SCHEDULE:
        steps[step](n)
    for n in range(len(CHUNKS)):
        for d in range(n_x):
            stage6_arrival(n, d).wait_recv()

    for d in order:
        a2a(d, csend, ret, a1_s, a1_r).wait_send()
        a2a(d, outg, arr, a2_s, a2_r).wait_send()
    for n in range(len(CHUNKS)):
        for d in order:
            stage3(n, d).wait_send()
            stage4(n, d).wait_send()
        for d in range(1, n_x):
            stage2(n, d).wait_send()
            stage5(n, d).wait_send()
        for d in range(n_x):
            stage6(n, d).wait_send()


def finish_kernel(n_x, n_gy, scale, ov, gi, ag, owned_out, gin_out, gw_out, gws, sem_big, sem_gw):
    plan, _, _ = chunk_plan(n_x, n_gy)
    copies = [pltpu.make_async_copy(gi.at[pl.ds(4 * n, 4)], gin_out.at[pl.ds(4 * n, 4)], sem_big.at[n]) for n in range(4)]
    copies.append(pltpu.make_async_copy(ov, owned_out, sem_big.at[4]))
    for copy in copies:
        copy.start()
    eye = as_bf(iota2((128, 128), 0) == iota2((128, 128), 1))
    for tap in range(TAPS):
        rows = jnp.concatenate(
            [
                ag[c, q, tile_of(plan, half, tap)]
                for c in range(2)
                for q in range(n_x)
                for half in range(128 // n_x // 16)
            ],
            0,
        )
        gws[tap] = dot_nt(eye, rows) * scale
        copy = pltpu.make_async_copy(gws.at[tap], gw_out.at[tap], sem_gw.at[tap])
        copy.start()
        copies.append(copy)
    for copy in copies:
        copy.wait()


def on_device(n_gx, n_gy, features, occupancy, weight, owner, cotangent):
    cap = cotangent.shape[2] // n_gy
    n_x = n_gx // 2
    rows2 = 128 // n_x
    _, tiles, per = chunk_plan(n_x, n_gy)
    slots_n = n_gy * cap

    V = pltpu.VMEM
    D = pltpu.SemaphoreType.DMA
    nc = len(CHUNKS)
    scratch = [
        V((17, 17, 64, 128), BF),
        V((17, 256, 1152), BF),
        V((16, 4, 256, 128), BF),
        V((8, 256, 128), BF),
        V((128, 16, 256), BF),
        V((slots_n, 16384), BF),
        V((slots_n, 64, 256), BF),
        V((slots_n, 64, 256), BF),
        V((slots_n, 64, 256), BF),
        V((slots_n, 64, 256), BF),
        V((TAPS * 128, 256), BF),
        V((9, 256, 256), BF),
        V((9, 32, 256), BF),
        V((8, 32, 256), BF),
        V((2, 9, 256, 512), BF),
        V((256, 2048), BF),
        V((16, 64, 128), BF),
        V((16, 64, 128), BF),
        V((256, TAPS * 128), F32),
        V((128, TAPS * 128), BF),
        V((128, TAPS * 128), BF),
        V((n_x, rows2, TAPS * 128), BF),
        V((n_x, rows2, TAPS * 128), BF),
        V((tiles, 16, 128), BF),
        V((n_gy, per, 16, 128), BF),
        V((4, 128, 256), BF),
        V((2, 256, 256), BF),
        V((256, 256), BF),
        V((4, 256, 256), BF),
        V((128, 128), BF),
        pltpu.SMEM((32,), jnp.int32),
        pltpu.SMEM((slots_n,), jnp.int32),
        D((16,)), D((2,)), D((2,)),
        D((16,)), D((16,)), D((16,)), D((16,)),
        D((3,)), D((3,)), D((3,)), D((3,)),
        D((nc,)), D((nc,)), D((nc, n_x)), D((nc, n_x)),
        D((nc, 16)), D((nc, 16)), D((nc, 16)), D((nc, 16)),
        D((nc, n_x)), D((nc, n_x)), D((nc, n_x)), D((nc, n_x)),
    ]

    def body(*refs):
        kernel(n_gx, n_gy, cap, *refs)

    def finish(*refs):
        finish_kernel(n_x, n_gy, float(8 * 8 * 32 * n_gx * n_gy) ** -0.5, *refs)

    smem = pl.BlockSpec(memory_space=pltpu.SMEM)
    vmem = pl.BlockSpec(memory_space=pltpu.VMEM)
    anywhere = pl.BlockSpec(memory_space=pl.ANY)
    parts = pl.pallas_call(
        body,
        out_shape=(
            V((slots_n, 16384), BF),
            V((16, 16, 64, 128), BF),
            V((2, n_x, tiles, 16, 128), BF),
        ),
        in_specs=[smem, vmem, anywhere, anywhere, anywhere],
        out_specs=[vmem] * 3,
        scratch_shapes=scratch,
        compiler_params=pltpu.CompilerParams(
            collective_id=0, has_side_effects=True, vmem_limit_bytes=50 * 1024 * 1024
        ),
        cost_estimate=pl.CostEstimate(
            flops=12_000_000_000, bytes_accessed=20_000_000, transcendentals=0
        ),
    )(owner.reshape(32), occupancy, features, weight.reshape(TAPS * 128, 256), cotangent)
    parts = [pltpu.with_memory_space_constraint(part, pltpu.VMEM) for part in parts]
    owned, gin, gw = pl.pallas_call(
        finish,
        out_shape=(
            jax.ShapeDtypeStruct((slots_n, 16384), BF),
            jax.ShapeDtypeStruct(features.shape, BF),
            jax.ShapeDtypeStruct(weight.shape, F32),
        ),
        in_specs=[vmem] * 3,
        out_specs=[anywhere] * 3,
        scratch_shapes=[V(weight.shape, F32), D((5,)), D((TAPS,))],
        compiler_params=pltpu.CompilerParams(vmem_limit_bytes=10 * 1024 * 1024),
        cost_estimate=pl.CostEstimate(flops=500_000_000, bytes_accessed=10_000_000, transcendentals=0),
    )(*parts)
    return owned.reshape(cotangent.shape), gin, gw


def solution(mesh):
    n_gx, n_gy = mesh.shape["gx"], mesh.shape["gy"]

    def local(*args):
        return on_device(n_gx, n_gy, *args)

    in_specs = (
        P("gx", "gy", None, None),
        P("gx", "gy", None),
        P(),
        P("gx", "gy", None),
        P("gx", "gy", None, None),
    )
    out_specs = (P("gx", "gy", None, None), P("gx", "gy", None, None), P())
    return jax.shard_map(
        local, mesh=mesh, in_specs=in_specs, out_specs=out_specs, check_vma=False
    )
```

```python
import jax
import jax.numpy as jnp
from jax import lax
from jax.experimental import pallas as pl
from jax.experimental.pallas import tpu as pltpu
from jax.sharding import PartitionSpec as P

BF = jnp.bfloat16
F32 = jnp.float32
MESH = pl.DeviceIdType.MESH
TAPS = 27
CHUNKS = ((0, 8), (8, 16), (16, 27))
SCHEDULE = (
    ("send", 0), ("weight", 0), ("weight", 1), ("sum1", 0), ("weight", 2), ("sum1", 1),
    ("sum1", 2), ("sum2", 0), ("up", 0), ("grad", 0), ("sum2", 1), ("sum3", 0),
    ("grad", 1), ("sum2", 2), ("sum3", 1), ("grad", 2), ("back1", 0), ("sum3", 2),
    ("send", 1), ("send", 2), ("back1", 1), ("grad", 3), ("grad", 4), ("back2", 0),
    ("back1", 2), ("grad", 5), ("grad", 6), ("back2", 1), ("grad", 7), ("back2", 2),
    ("owned", 0),
)
FAR_FIRST = (10, 6, 9, 11, 14, 5, 7, 13, 15, 2, 8, 1, 3, 4, 12)


def iota2(shape, dim):
    return lax.broadcasted_iota(jnp.int32, shape, dim)


def as_bf(cond):
    return jnp.where(cond, 1.0, 0.0).astype(F32).astype(BF)


def dot(a, b):
    return jnp.dot(a, b, preferred_element_type=F32)


def dot_nt(a, b):
    return lax.dot_general(a, b, (((1,), (1,)), ((), ())), preferred_element_type=F32)


def chunk_plan(n_x, n_gy):
    halves = 128 // n_x // 16
    plan, first, mine = [], 0, 0
    for t0, t1 in CHUNKS:
        used = halves * (t1 - t0)
        per = -(-used // n_gy)
        plan.append((used, per, first, mine))
        first += per * n_gy
        mine += per
    return plan, first, mine


def tile_of(plan, half, tap):
    for (t0, t1), (_, _, first, _) in zip(CHUNKS, plan):
        if t0 <= tap < t1:
            return first + half * (t1 - t0) + tap - t0


def partner(j, d):
    total, bit = 0, 1
    while bit <= 8:
        b = (j // bit) % 2
        total = total + bit * (1 - b if d & bit else b)
        bit *= 2
    return total


def row_coords(rows):
    return rows // 128, (rows // 16) % 8, (rows // 4) % 4, rows % 4


def kernel(
    n_gx, n_gy, cap,
    owner_ref, occ_ref, feat, weight, cot,
    ov, gi, ag,
    fp, pt, mk, act, bk, cv, csend, ret, outg, arr, wv, ub, yhu, ysu, uu, upt,
    xs, ys, dwf, s1s, s1r, s2s, s2r, s3s, s3r, pk, pc, po, qs, pysel,
    slot_ref, inv_ref, sem_feat, sem_in, sem_loc,
    a1_s, a1_r, a2_s, a2_r, h_s, h_r, u_s, u_r,
    r1_s, r1_r, r2_s, r2_r, r3_s, r3_r, g4_s, g4_r, g5_s, g5_r, g6_s, g6_r,
):
    n_x = n_gx // 2
    i = lax.axis_index("gx")
    j = lax.axis_index("gy")
    xq = i // 2
    core = lax.rem(i, 2)
    sib = 2 * xq + 1 - core
    nxt_i, prv_i = lax.rem(i + 1, n_gx), lax.rem(i + n_gx - 1, n_gx)
    nxt_j, prv_j = lax.rem(j + 1, n_gy), lax.rem(j + n_gy - 1, n_gy)

    cot_copy = pltpu.make_async_copy(cot.at[0, 0], cv, sem_in.at[0])
    cot_copy.start()

    def feat_copy(x):
        return pltpu.make_async_copy(feat.at[x], fp.at[x + 1, pl.ds(1, 16)], sem_feat.at[x])

    for x in range(15, -1, -1):
        feat_copy(x).start()
    w_copy = pltpu.make_async_copy(weight, wv, sem_in.at[1])
    w_copy.start()

    barrier = pltpu.get_barrier_semaphore()
    order = [d for d in FAR_FIRST if d < n_gy]
    peer_j = {d: partner(j, d) for d in order}
    peers = [(i, peer_j[d]) for d in order]
    peers += [(lax.rem(i + d, n_gx), j) for d in range(2, n_gx - 1, 2)]
    peers += [(nxt_i, j), (prv_i, j), (nxt_i, nxt_j), (prv_i, prv_j)]
    for peer in peers:
        pl.semaphore_signal(barrier, inc=1, device_id=peer, device_id_type=MESH)

    r, c = iota2((128, 256), 0), iota2((128, 256), 1)
    _, bz, vy, vz = row_coords(r)
    oz = 4 * bz + vz
    for kz in range(3):
        pk[kz] = as_bf((vy == c // 64) & (2 * oz + kz - 1 == c % 64))
    pk[3] = as_bf((vy == c // 64) & (oz == (c % 64) // 2))
    r, c = iota2((256, 256), 0), iota2((256, 256), 1)
    pc[0] = as_bf((r // 16 == c % 16) & (r % 16 == c // 16))
    pc[1] = as_bf(r == c)
    _, cbz, cvy, cvz = row_coords(c % 128)
    po[...] = as_bf((cvy == r // 64) & (8 * cbz + 2 * cvz + c // 128 == r % 64))
    rby, rbz, rvy, rvz = row_coords(r)
    cby, cbz, cvy, cvz = row_coords(c)
    roz, coz = 4 * rbz + rvz, 4 * cbz + cvz
    roy, coy = 4 * rby + rvy, 4 * cby + cvy
    qs[0] = as_bf((roy == coy) & (roz + 1 == coz))
    qs[1] = as_bf((roy + 1 == coy) & (roz == coz))
    qs[2] = as_bf((roy + 1 == coy) & (roz + 1 == coz))
    r, c = iota2((256, 128), 0), iota2((256, 128), 1)
    rby, rbz, rvy, rvz = row_coords(r)
    top = (4 * rby + rvy == 7) & (c < 32)
    qs[3, :, 0:128] = as_bf(top & (4 * rbz + rvz == c))
    qs[3, :, 128:256] = as_bf(top & (4 * rbz + rvz + 1 == c))
    r, c = iota2((128, 128), 0), iota2((128, 128), 1)
    _, cbz, cvy, cvz = row_coords(c)
    pysel[...] = as_bf((r < 32) & (cvy == 0) & (4 * cbz + cvz == r))

    def remote(src, dst, s_sem, r_sem, to):
        return pltpu.make_async_remote_copy(
            src_ref=src, dst_ref=dst, send_sem=s_sem, recv_sem=r_sem,
            device_id=to, device_id_type=MESH,
        )

    def a2a(d, src, dst, s_sem, r_sem):
        to = peer_j[d]
        return remote(
            src.at[pl.ds(to * cap, cap)], dst.at[pl.ds(j * cap, cap)], s_sem.at[d], r_sem.at[d], (i, to)
        )

    def a2a_arrival(d, src, dst, s_sem, r_sem):
        frm = peer_j[d]
        here = pl.ds(frm * cap, cap)
        return remote(src.at[here], dst.at[here], s_sem.at[d], r_sem.at[d], (i, frm))

    def occ_row(x, y):
        return occ_ref[x, pl.ds(y, 1), :].astype(F32)

    def lanes_of(rows):
        return jnp.concatenate(rows, 1)

    def wide(row):
        return jnp.broadcast_to(row, (16, 256)).astype(BF)

    def masked_rows(mat, row):
        rows = mat.shape[0]
        m = wide(row)
        return (mat.reshape(rows // 16, 16, 256) * m[None]).reshape(rows, 256)

    feat_copy(15).wait()
    for by in range(2):
        for py in range(2):
            row = lanes_of([occ_row(15, 8 * by + 2 * v + py) for v in range(4)])
            rhs = jnp.concatenate([fp[16, 1 + 8 * by + 2 * v + py] for v in range(4)], 0)
            res = dot(masked_rows(pc[1], row), rhs).astype(BF)
            for v in range(4):
                xs[8 * by + 2 * v + py] = res[64 * v : 64 * v + 64]

    for x in range(14, -1, -1):
        feat_copy(x).wait()

    def mask_y(x, carry):
        row = lanes_of([occ_row(x, 9 + 2 * v) for v in range(4)])
        rhs = jnp.concatenate([fp[x + 1, 10 + 2 * v] for v in range(4)], 0)
        ys[x] = dot(masked_rows(pc[1, 192:256, :], row), rhs).astype(BF)
        return carry

    lax.fori_loop(0, 16, mask_y, 0, unroll=4)
    pl.semaphore_wait(barrier, len(peers))
    halo_x = remote(xs, fp.at[0, pl.ds(1, 16)], h_s.at[0], h_r.at[0], (nxt_i, j))
    halo_y = remote(ys, fp.at[pl.ds(1, 16), 0], h_s.at[1], h_r.at[1], (i, nxt_j))
    halo_c = remote(ys.at[15], fp.at[0, 0], h_s.at[2], h_r.at[2], (nxt_i, nxt_j))
    halo_y.start()
    halo_x.start()
    halo_c.start()
    cot_copy.wait()

    def cot_step(n, carry):
        t, vg = n // 4, n % 4
        rhs = jnp.concatenate(
            [
                cv[pl.ds(pl.multiple_of(16 * t, 16), 16), pl.ds(pl.multiple_of(4096 * vg + 256 * v, 256), 256)]
                for v in range(16)
            ],
            0,
        )
        res = dot(pc[0], rhs).astype(BF).reshape(16, 16, 256)
        csend[pl.ds(16 * t, 16), pl.ds(pl.multiple_of(16 * vg, 16), 16), :] = res
        return carry

    lax.fori_loop(0, 12, cot_step, 0)

    for d in order:
        a2a(d, csend, ret, a1_s, a1_r).start()
    own1 = pltpu.make_async_copy(
        csend.at[pl.ds(j * cap, cap)], ret.at[pl.ds(j * cap, cap)], sem_loc.at[0]
    )
    own1.start()

    ones = jnp.ones((256, 128), F32).astype(BF)

    def prep(xp, by, ky, row, own):
        rhs = jnp.concatenate([fp[xp, 8 * by + 2 * v + ky] for v in range(4)], 0)
        with_mask = own and ky > 0
        if with_mask:
            rhs = jnp.concatenate([rhs, ones], 1)
        for kz in range(3):
            res = dot(masked_rows(pk[kz], row), rhs if kz > 0 or not with_mask else rhs[:, :128])
            col = (3 * ky + kz) * 128
            pt[xp, by * 128 : by * 128 + 128, col : col + 128] = res[:, :128].astype(BF)
            if with_mask and kz > 0:
                mk[xp - 1, 2 * (ky - 1) + kz - 1, by * 128 : by * 128 + 128, :] = res[:, 128:].astype(BF)

    def prep_own(x, carry):
        for by, ky in ((0, 1), (0, 2), (1, 0), (1, 1), (1, 2)):
            row = lanes_of([occ_row(x, 8 * by + 2 * v + ky - 1) for v in range(4)])
            prep(x + 1, by, ky, row, True)
        return carry

    lax.fori_loop(0, 16, prep_own, 0)

    def count_active(ox, carry):
        for by in range(2):
            total = jnp.zeros((1, 256), F32)
            for px in range(2):
                for py in range(2):
                    total = total + lanes_of([occ_row(2 * ox + px, 8 * by + 2 * v + py) for v in range(4)])
            count = dot(masked_rows(pk[3], total), ones)
            act[ox, by * 128 : by * 128 + 128, :] = jnp.where(count > 0.5, 1.0, 0.0).astype(BF)
        return carry

    lax.fori_loop(0, 8, count_active, 0)

    ok_x = jnp.where(i > 0, 1.0, 0.0).astype(F32)
    ok_y = jnp.where(j > 0, 1.0, 0.0).astype(F32)
    halo_x.wait()
    halo_y.wait()
    halo_c.wait()

    def prep_halo_y(x, carry):
        row = lanes_of([jnp.full((1, 64), ok_y, F32)] + [occ_row(x, 2 * v + 1) for v in range(3)])
        prep(x + 1, 0, 0, row, False)
        return carry

    lax.fori_loop(0, 16, prep_halo_y, 0)
    row_x = jnp.full((1, 256), ok_x, F32)
    corner = jnp.where(iota2((1, 256), 1) < 64, ok_x * ok_y, ok_x)
    for by in range(2):
        for ky in range(3):
            prep(0, by, ky, corner if (by == 0 and ky == 0) else row_x, False)

    w_copy.wait()

    def forward(ox, carry):
        lhs = jnp.concatenate([pt[2 * ox], pt[2 * ox + 1], pt[2 * ox + 2]], 1)
        acc = dot(lhs, wv[...])
        a = act[ox]
        a = jnp.concatenate([a, a], 1).astype(F32)
        bk[pl.ds(ox * 16, 16)] = (acc * a).astype(BF).reshape(16, 16, 256)
        return carry

    lax.fori_loop(0, 8, forward, 0)

    owners = [owner_ref[b] for b in range(32)]
    for b in range(32):
        slot = owners[b] * cap
        for earlier in range(b):
            slot = slot + jnp.where(owners[earlier] == owners[b], 1, 0)
        slot_ref[b] = slot

    def invert(s, carry):
        found = jnp.int32(0)
        for b in range(32):
            found = found + jnp.where(slot_ref[b] == s, (b // 16) * 64 + b % 16 + 1, 0)
        inv_ref[s] = found - 1
        return carry

    lax.fori_loop(0, n_gy * cap, invert, 0)

    def pack(s, carry):
        base = inv_ref[s]
        keep = jnp.where(base >= 0, 1.0, 0.0).astype(F32)
        at = jnp.maximum(base, 0)
        flag = jnp.full((16, 256), keep, F32).astype(BF)
        for vx in range(4):
            outg[s, vx * 16 : vx * 16 + 16, :] = bk[at + 16 * vx] * flag
        return carry

    lax.fori_loop(0, n_gy * cap, pack, 0)

    own1.wait()
    for d in order:
        a2a_arrival(d, csend, ret, a1_s, a1_r).wait_recv()

    def place(b, carry):
        s = slot_ref[b]
        bx, rest = b // 16, b % 16
        for vx in range(4):
            off = pl.multiple_of(rest * 16, 16)
            a = act[bx * 4 + vx, pl.ds(off, 16), :]
            a = jnp.concatenate([a, a], 1)
            ub[bx * 4 + vx, pl.ds(off, 16), :] = ret[s, vx * 16 : vx * 16 + 16, :] * a
        return carry

    lax.fori_loop(0, 32, place, 0)

    for ox in range(8):
        ysu[ox] = dot(pysel[...], ub[ox, 0:128, :])[0:32].astype(BF)
    up_x = remote(ub.at[0], ub.at[8], u_s.at[0], u_r.at[0], (prv_i, j))
    up_y = remote(ysu, yhu.at[pl.ds(0, 8)], u_s.at[1], u_r.at[1], (i, prv_j))
    up_c = remote(ysu.at[0], yhu.at[8], u_s.at[2], u_r.at[2], (prv_i, prv_j))
    up_x.start()
    up_y.start()
    up_c.start()

    own2 = pltpu.make_async_copy(
        outg.at[pl.ds(j * cap, cap)], arr.at[pl.ds(j * cap, cap)], sem_loc.at[1]
    )
    own2.start()

    def send(n):
        for d in order[(0, 4, 9)[n] : (4, 9, 15)[n]]:
            a2a(d, outg, arr, a2_s, a2_r).start()

    for ox in range(8):
        upt[:, ox * 256 : ox * 256 + 256] = dot_nt(pc[1], ub[ox]).astype(BF)

    mine = pl.multiple_of(core * 128, 128)
    other = pl.multiple_of(128 - core * 128, 128)

    rows2 = 128 // n_x
    plan, _, _ = chunk_plan(n_x, n_gy)

    def columns(n):
        return slice(CHUNKS[n][0] * 128, CHUNKS[n][1] * 128)

    def tap_rows(tap):
        kx, col = tap // 9, (tap % 9) * 128
        return jnp.concatenate([pt[2 * ox + kx, :, col : col + 128] for ox in range(8)], 0)

    def stage1(n):
        cols = columns(n)
        return remote(s1s.at[:, cols], s1r.at[:, cols], r1_s.at[n], r1_r.at[n], (sib, j))

    def weight_chunk(n):
        t0, t1 = CHUNKS[n]
        for tap in range(t0, t1, 2):
            rhs = tap_rows(tap)
            if tap + 1 < t1:
                rhs = jnp.concatenate([rhs, tap_rows(tap + 1)], 1)
            dwf[:, tap * 128 : tap * 128 + rhs.shape[1]] = dot(upt[...], rhs)
        cols = columns(n)
        s1s[:, cols] = dwf[pl.ds(other, 128), cols].astype(BF)
        stage1(n).start()

    def stage2(n, d):
        cols = columns(n)
        to = lax.rem(xq + d, n_x)
        return remote(s2s.at[to, :, cols], s2r.at[xq, :, cols], r2_s.at[n, d], r2_r.at[n, d], (2 * to + core, j))

    def stage2_arrival(n, d):
        cols = columns(n)
        frm = lax.rem(xq - d + n_x, n_x)
        return remote(s2s.at[frm, :, cols], s2r.at[frm, :, cols], r2_s.at[n, d], r2_r.at[n, d], (2 * frm + core, j))

    def after1(n):
        cols = columns(n)
        stage1(n).wait()
        for q in range(n_x):
            at = pl.multiple_of(mine + q * rows2, 16)
            mid = dwf[pl.ds(at, rows2), cols] + s1r[q * rows2 : (q + 1) * rows2, cols].astype(F32)
            dwf[pl.ds(at, rows2), cols] = mid
            s2s[q, :, cols] = mid.astype(BF)
        for d in range(1, n_x):
            stage2(n, d).start()

    def stage3(n, d):
        _, per, first, own = plan[n]
        to = peer_j[d]
        return remote(
            s3s.at[pl.ds(first + to * per, per)], s3r.at[j, pl.ds(own, per)],
            r3_s.at[n, d], r3_r.at[n, d], (i, to),
        )

    def stage3_arrival(n, d):
        _, per, first, own = plan[n]
        frm = peer_j[d]
        return remote(
            s3s.at[pl.ds(first + frm * per, per)], s3r.at[frm, pl.ds(own, per)],
            r3_s.at[n, d], r3_r.at[n, d], (i, frm),
        )

    def after2(n):
        used, per, first, _ = plan[n]
        t0, t1 = CHUNKS[n]
        cols = columns(n)
        for d in range(1, n_x):
            stage2_arrival(n, d).wait_recv()
        for half in range(rows2 // 16):
            at = pl.multiple_of(mine + xq * rows2 + half * 16, 16)
            total = dwf[pl.ds(at, 16), cols]
            for d in range(1, n_x):
                frm = lax.rem(xq + d, n_x)
                total = total + s2r[frm, half * 16 : half * 16 + 16, cols].astype(F32)
            total = total.astype(BF)
            for t in range(t1 - t0):
                s3s[first + half * (t1 - t0) + t] = total[:, t * 128 : t * 128 + 128]
        for t in range(first + used, first + per * n_gy):
            s3s[t] = jnp.zeros((16, 128), BF)
        for d in order:
            stage3(n, d).start()

    def stage4(n, d):
        _, per, first, _ = plan[n]
        here = ag.at[core, xq, pl.ds(first + j * per, per)]
        return remote(here, here, g4_s.at[n, d], g4_r.at[n, d], (i, peer_j[d]))

    def stage4_arrival(n, d):
        _, per, first, _ = plan[n]
        here = ag.at[core, xq, pl.ds(first + peer_j[d] * per, per)]
        return remote(here, here, g4_s.at[n, d], g4_r.at[n, d], (i, peer_j[d]))

    def after3(n):
        _, per, first, own = plan[n]
        for d in order:
            stage3_arrival(n, d).wait_recv()
        total = s3s[pl.ds(first + j * per, per)].astype(F32)
        for d in order:
            total = total + s3r[peer_j[d], own : own + per].astype(F32)
        ag[core, xq, pl.ds(first + j * per, per)] = total.astype(BF)
        for d in order:
            stage4(n, d).start()

    def block(c, q, n):
        used, _, first, _ = plan[n]
        return ag.at[c, q, first : first + used]

    def stage5(n, d):
        to = lax.rem(xq + d, n_x)
        here = block(core, xq, n)
        return remote(here, here, g5_s.at[n, d], g5_r.at[n, d], (2 * to + core, j))

    def stage5_arrival(n, d):
        frm = lax.rem(xq - d + n_x, n_x)
        here = block(core, frm, n)
        return remote(here, here, g5_s.at[n, d], g5_r.at[n, d], (2 * frm + core, j))

    def stage6(n, d):
        here = block(core, lax.rem(xq - d + n_x, n_x), n)
        return remote(here, here, g6_s.at[n, d], g6_r.at[n, d], (sib, j))

    def stage6_arrival(n, d):
        here = block(1 - core, lax.rem(xq - d + n_x, n_x), n)
        return remote(here, here, g6_s.at[n, d], g6_r.at[n, d], (sib, j))

    def after4(n):
        for d in order:
            stage4_arrival(n, d).wait_recv()
        for d in range(1, n_x):
            stage5(n, d).start()
        stage6(n, 0).start()

    def after5(n):
        for d in range(1, n_x):
            stage5_arrival(n, d).wait_recv()
            stage6(n, d).start()

    okn_x = jnp.where(i < n_gx - 1, 1.0, 0.0).astype(F32)
    okn_y = jnp.where(j < n_gy - 1, 1.0, 0.0).astype(F32)

    def shifts(ox, carry):
        last = jnp.where(ox == 8, okn_x, 1.0).astype(F32)
        base = (ub[ox].astype(F32) * last).astype(BF)
        halo = (yhu[ox].astype(F32) * (last * okn_y)).astype(BF)
        halo = jnp.concatenate([halo, jnp.zeros((96, 256), BF)], 0)
        uu[0, ox, :, 0:256] = base
        uu[0, ox, :, 256:512] = dot(qs[0], base).astype(BF)
        uu[1, ox, :, 0:256] = (dot(qs[1], base) + dot(qs[3, :, 0:128], halo)).astype(BF)
        uu[1, ox, :, 256:512] = (dot(qs[2], base) + dot(qs[3, :, 128:256], halo)).astype(BF)
        return carry

    def shift_all(n):
        up_x.wait()
        up_y.wait()
        up_c.wait()
        lax.fori_loop(0, 9, shifts, 0, unroll=3)

    lists = (((1, 0),), ((2, 0), (0, 1)))

    def grad_in(ox, carry):
        for px in range(2):
            for py in range(2):
                both, odd = None, None
                for a, sx in lists[px]:
                    for b, sy in lists[py]:
                        k = 9 * a + 3 * b
                        one = dot_nt(uu[sy, ox + sx, :, 0:256], wv[(k + 1) * 128 : (k + 3) * 128, :])
                        two = dot_nt(uu[sy, ox + sx, :, 256:512], wv[k * 128 : (k + 1) * 128, :])
                        both = one if both is None else both + one
                        odd = two if odd is None else odd + two
                m0 = mk[2 * ox + px, 2 * py].astype(F32)
                m1 = mk[2 * ox + px, 2 * py + 1].astype(F32)
                g0 = (both[:, :128] * m0).astype(BF)
                g1 = ((both[:, 128:] + odd) * m1).astype(BF)
                rhs = jnp.concatenate(
                    [
                        jnp.concatenate([g0[:128], g1[:128]], 0),
                        jnp.concatenate([g0[128:], g1[128:]], 0),
                    ],
                    1,
                )
                res = dot(po[...], rhs).astype(BF)
                for by in range(2):
                    for v in range(4):
                        gi[2 * ox + px, 8 * by + 2 * v + py] = res[64 * v : 64 * v + 64, 128 * by : 128 * by + 128]
        return carry

    def one_grad(n):
        grad_in(n, 0)

    def owned_step(n, carry):
        t, vg = n // 4, n % 4
        rhs = arr[pl.ds(16 * t, 16), pl.ds(pl.multiple_of(16 * vg, 16), 16), :].reshape(256, 256)
        res = dot(pc[0], rhs).astype(BF)
        for v in range(16):
            ov[pl.ds(pl.multiple_of(16 * t, 16), 16), pl.ds(pl.multiple_of(4096 * vg + 256 * v, 256), 256)] = res[16 * v : 16 * v + 16]
        return carry

    def owned(n):
        own2.wait()
        for d in order:
            a2a_arrival(d, outg, arr, a2_s, a2_r).wait_recv()
        lax.fori_loop(0, 12, owned_step, 0, unroll=2)

    steps = dict(
        weight=weight_chunk, sum1=after1, sum2=after2, sum3=after3, back1=after4, back2=after5,
        up=shift_all, grad=one_grad, send=send, owned=owned,
    )
    for step, n in SCHEDULE:
        steps[step](n)
    for n in range(len(CHUNKS)):
        for d in range(n_x):
            stage6_arrival(n, d).wait_recv()

    for d in order:
        a2a(d, csend, ret, a1_s, a1_r).wait_send()
        a2a(d, outg, arr, a2_s, a2_r).wait_send()
    for n in range(len(CHUNKS)):
        for d in order:
            stage3(n, d).wait_send()
            stage4(n, d).wait_send()
        for d in range(1, n_x):
            stage2(n, d).wait_send()
            stage5(n, d).wait_send()
        for d in range(n_x):
            stage6(n, d).wait_send()


def finish_kernel(n_x, n_gy, scale, ov, gi, ag, owned_out, gin_out, gw_out, gws, sem_big, sem_gw):
    plan, _, _ = chunk_plan(n_x, n_gy)
    copies = [pltpu.make_async_copy(gi.at[pl.ds(4 * n, 4)], gin_out.at[pl.ds(4 * n, 4)], sem_big.at[n]) for n in range(4)]
    copies.append(pltpu.make_async_copy(ov, owned_out, sem_big.at[4]))
    for copy in copies:
        copy.start()
    eye = as_bf(iota2((128, 128), 0) == iota2((128, 128), 1))
    for tap in range(TAPS):
        rows = jnp.concatenate(
            [
                ag[c, q, tile_of(plan, half, tap)]
                for c in range(2)
                for q in range(n_x)
                for half in range(128 // n_x // 16)
            ],
            0,
        )
        gws[tap] = dot_nt(eye, rows) * scale
        copy = pltpu.make_async_copy(gws.at[tap], gw_out.at[tap], sem_gw.at[tap])
        copy.start()
        copies.append(copy)
    for copy in copies:
        copy.wait()


def on_device(n_gx, n_gy, features, occupancy, weight, owner, cotangent):
    cap = cotangent.shape[2] // n_gy
    n_x = n_gx // 2
    rows2 = 128 // n_x
    _, tiles, per = chunk_plan(n_x, n_gy)
    slots_n = n_gy * cap

    V = pltpu.VMEM
    D = pltpu.SemaphoreType.DMA
    nc = len(CHUNKS)
    scratch = [
        V((17, 17, 64, 128), BF),
        V((17, 256, 1152), BF),
        V((16, 4, 256, 128), BF),
        V((8, 256, 128), BF),
        V((128, 16, 256), BF),
        V((slots_n, 16384), BF),
        V((slots_n, 64, 256), BF),
        V((slots_n, 64, 256), BF),
        V((slots_n, 64, 256), BF),
        V((slots_n, 64, 256), BF),
        V((TAPS * 128, 256), BF),
        V((9, 256, 256), BF),
        V((9, 32, 256), BF),
        V((8, 32, 256), BF),
        V((2, 9, 256, 512), BF),
        V((256, 2048), BF),
        V((16, 64, 128), BF),
        V((16, 64, 128), BF),
        V((256, TAPS * 128), F32),
        V((128, TAPS * 128), BF),
        V((128, TAPS * 128), BF),
        V((n_x, rows2, TAPS * 128), BF),
        V((n_x, rows2, TAPS * 128), BF),
        V((tiles, 16, 128), BF),
        V((n_gy, per, 16, 128), BF),
        V((4, 128, 256), BF),
        V((2, 256, 256), BF),
        V((256, 256), BF),
        V((4, 256, 256), BF),
        V((128, 128), BF),
        pltpu.SMEM((32,), jnp.int32),
        pltpu.SMEM((slots_n,), jnp.int32),
        D((16,)), D((2,)), D((2,)),
        D((16,)), D((16,)), D((16,)), D((16,)),
        D((3,)), D((3,)), D((3,)), D((3,)),
        D((nc,)), D((nc,)), D((nc, n_x)), D((nc, n_x)),
        D((nc, 16)), D((nc, 16)), D((nc, 16)), D((nc, 16)),
        D((nc, n_x)), D((nc, n_x)), D((nc, n_x)), D((nc, n_x)),
    ]

    def body(*refs):
        kernel(n_gx, n_gy, cap, *refs)

    def finish(*refs):
        finish_kernel(n_x, n_gy, float(8 * 8 * 32 * n_gx * n_gy) ** -0.5, *refs)

    smem = pl.BlockSpec(memory_space=pltpu.SMEM)
    vmem = pl.BlockSpec(memory_space=pltpu.VMEM)
    anywhere = pl.BlockSpec(memory_space=pl.ANY)
    parts = pl.pallas_call(
        body,
        out_shape=(
            V((slots_n, 16384), BF),
            V((16, 16, 64, 128), BF),
            V((2, n_x, tiles, 16, 128), BF),
        ),
        in_specs=[smem, vmem, anywhere, anywhere, anywhere],
        out_specs=[vmem] * 3,
        scratch_shapes=scratch,
        compiler_params=pltpu.CompilerParams(
            collective_id=0, has_side_effects=True, vmem_limit_bytes=50 * 1024 * 1024
        ),
        cost_estimate=pl.CostEstimate(
            flops=12_000_000_000, bytes_accessed=20_000_000, transcendentals=0
        ),
    )(owner.reshape(32), occupancy, features, weight.reshape(TAPS * 128, 256), cotangent)
    parts = [pltpu.with_memory_space_constraint(part, pltpu.VMEM) for part in parts]
    owned, gin, gw = pl.pallas_call(
        finish,
        out_shape=(
            jax.ShapeDtypeStruct((slots_n, 16384), BF),
            jax.ShapeDtypeStruct(features.shape, BF),
            jax.ShapeDtypeStruct(weight.shape, F32),
        ),
        in_specs=[vmem] * 3,
        out_specs=[anywhere] * 3,
        scratch_shapes=[V(weight.shape, F32), D((5,)), D((TAPS,))],
        compiler_params=pltpu.CompilerParams(vmem_limit_bytes=10 * 1024 * 1024),
        cost_estimate=pl.CostEstimate(flops=500_000_000, bytes_accessed=10_000_000, transcendentals=0),
    )(*parts)
    return owned.reshape(cotangent.shape), gin, gw


def solution(mesh):
    n_gx, n_gy = mesh.shape["gx"], mesh.shape["gy"]

    def local(*args):
        return on_device(n_gx, n_gy, *args)

    in_specs = (
        P("gx", "gy", None, None),
        P("gx", "gy", None),
        P(),
        P("gx", "gy", None),
        P("gx", "gy", None, None),
    )
    out_specs = (P("gx", "gy", None, None), P("gx", "gy", None, None), P())
    return jax.shard_map(
        local, mesh=mesh, in_specs=in_specs, out_specs=out_specs, check_vma=False
    )
```
